256 devices in a mesh: grp: 8 (over y, core), clu: 32 (over z, x).
Axes of the slice: x: 4, y: 4, z: 8, core: 2. Of those that a mesh axis runs over, the one named last changes fastest.
Arguments:
- near_blocks: bfloat16 [2048, 6, 256, 256], P(('grp', 'clu')), may hold values from -6 to 6
- diag_blocks: bfloat16 [2048, 256, 256], P(('grp', 'clu')), may hold values from -6 to 6
- bases: bfloat16 [2048, 256, 256], P(('grp', 'clu')), may hold values from -0.375 to 0.375
- diag_inverses: float32 [2048, 128, 128], P(('grp', 'clu')), may hold values from -0.5 to 0.5
- col_device: int32 [2048, 6], P(('grp', 'clu')), may hold values from 0 to 31, all different within a row; in each aligned block of 8 rows (0 to 7, 8 to 15, ...) at most 2 rows name the same one
- col_local: int32 [2048, 6], P(('grp', 'clu')), may hold values from 0 to 7
- ranks: int32 [2048], P(('grp', 'clu')), may hold values from 64 to 128
- parent_group: int32 [2048, 1], P(('grp', 'clu')), may hold values from 0 to 7; in each aligned block of 8 rows (0 to 7, 8 to 15, ...) no two rows name the same one
Outputs:
- reduced_near: bfloat16 [256, 32, 2, 128, 128], P(('grp', 'clu'))
- merged: bfloat16 [1024, 2, 128, 128], P(('grp', 'clu'))
The draws below stay inside these ranges and needn't reach their ends.
Inputs may be any that keep to these rules, and one draw needn't show every extreme that they name: `col_device`: within the rows of one device, no device of the subtree is named by more than 2 blocks, and the entries of one row are distinct. `parent_group`: the clusters of one device name each subtree exactly 1 times.
All inputs are finite; a program needn't handle non-finite values.
Results may differ from the reference program's by a relative error of at most 0.0076.
Values may be sent and summed in bfloat16 or wider, within the bound.
No kernel may reach another device: no remote copies, remote signals or barrier semaphores. Data moves between devices by JAX's collectives and lax.ppermute only.
A program may use at most 128 MiB of HBM per device.

```python
import math
import jax
import jax.numpy as jnp
import numpy as np
from jax import lax

BLOCK = 256
SKEL = 128
REDUND = 128
CLDEV = 8
NEAR = 6
CAP = 2
MPG = 1
CLUSTERS = 2048
PARENTS = 1024
N_GRP = 8
N_CLU = 32


def touch_ends(entries, stream_key, low, top_value):
    longest = entries.shape.index(max(entries.shape))
    spots = []
    for shift in (0, 1):
        where = [jax.random.randint(jax.random.fold_in(stream_key, axis), (), 0, length) for axis, length in enumerate(entries.shape)]
        where[longest] = (where[longest] + shift) % entries.shape[longest]
        spots.append(tuple(where))
    return entries.at[spots[0]].set(low).at[spots[1]].set(top_value)


def steps_of(rng, extent, split, least, high):
    gain = 1.0
    for axis_at, shards_of in split:
        steps = jax.random.uniform(jax.random.fold_in(jax.random.fold_in(rng, 6), axis_at), (shards_of,), jnp.float32, least / len(split), high / len(split))
        gain = gain * jnp.repeat(jnp.exp(steps), extent[axis_at] // shards_of).reshape((-1,) + (1,) * (len(extent) - 1 - axis_at))
    return gain


def shared_out(rng, own, number, rows, amount, top, reach, skew):
    order = jax.random.permutation(rng, amount)
    heavy_load, ordinary = load_shares(amount, rows * top, reach, skew, True), load_shares(amount, rows * top, reach, skew, False)
    places = jnp.arange(amount)

    def named(tallies, rotation):
        used = int((tallies > 0).sum())
        fixed = max(1, used // 4)
        moved = fixed + (places - fixed + rotation * (used - fixed)) % max(1, amount - fixed)
        return jnp.zeros((amount,), jnp.int32).at[order[jnp.where(places < fixed, places, moved)]].set(jnp.asarray(tallies, jnp.int32))

    tallies = jnp.where(number % 4 == 0, named(heavy_load, number // 4), named(ordinary, number - number // 4 - 1))
    mixed = jax.random.permutation(jax.random.fold_in(own, 3), amount)
    source_of, receiver = mixed[0:amount // 2 * 2:2], mixed[1:amount // 2 * 2:2]
    slack = jnp.minimum(tallies[source_of] - 1, reach - tallies[receiver]) // 2
    slack = jnp.where((source_of == order[0]) | (receiver == order[0]) | (tallies[receiver] == 0), 0, jnp.maximum(slack, 0))
    moved = jax.random.randint(jax.random.fold_in(own, 4), (amount // 2,), 0, 1 << 20) % (slack + 1)
    tallies = tallies.at[source_of].add(-moved).at[receiver].add(moved)
    labels = jnp.searchsorted(jnp.cumsum(tallies), jnp.arange(rows * top), side="right").astype(jnp.int32)
    grid = labels.reshape(top, rows).T
    grid = grid[jax.random.permutation(jax.random.fold_in(own, 1), rows)]
    rotation = jax.random.randint(jax.random.fold_in(own, 2), (rows, 1), 0, top)
    return jnp.take_along_axis(grid, (jnp.arange(top)[None, :] + rotation) % top, axis=1)


def load_shares(number_of, total, most, slope, full):
    portions = [(1 << 20) // math.isqrt(rank ** slope) + 1 for rank in range(1, number_of + 1)]
    largest = most if full else min(most, max(-(-total // number_of), total * portions[0] // sum(portions)))
    least = 1 if total - largest >= number_of - 1 else 0
    holding, surplus = [largest] + [least] * (number_of - 1), total - largest - least * (number_of - 1)
    while surplus > 0:
        movable = [i for i in range(1, number_of) if holding[i] < largest] or [i for i in range(1, number_of) if holding[i] < most]
        pool, budget = sum([portions[i] for i in movable]), surplus
        for i in movable:
            more = min(most - holding[i], max(1, budget * portions[i] // pool), surplus)
            holding[i] = holding[i] + more
            surplus = surplus - more
    return np.array(holding)


def gaussian(own_key, extent, scale, most, pieces=(), kind=jnp.bfloat16):
    factor_of = steps_of(own_key, extent, pieces, -0.22, 0.18) if pieces else 1.0
    values = jax.random.normal(own_key, extent, jnp.float32) * scale * factor_of
    return jnp.minimum(jnp.maximum(values, -most), most).astype(kind)


def setup_inputs(seed: int = 0) -> dict:
    key_of = jax.random.split(jax.random.key(seed), 9)
    near_blocks = gaussian(key_of[0], (CLUSTERS, NEAR, BLOCK, BLOCK), 1.0, 6.0, ((0, 256),))
    diag_blocks = gaussian(key_of[1], (CLUSTERS, BLOCK, BLOCK), 1.0, 6.0, ((0, 256),))
    bases = gaussian(key_of[2], (CLUSTERS, BLOCK, BLOCK), BLOCK ** -0.5, 0.375, ((0, 256),))
    diag_inverses = gaussian(key_of[3], (CLUSTERS, REDUND, REDUND), REDUND ** -0.5, 0.5, ((0, 256),), jnp.float32)
    col_device_keys = jax.random.split(jax.random.fold_in(key_of[4], 1), CLUSTERS // CLDEV)
    col_device_turns = jax.random.permutation(jax.random.fold_in(key_of[4], 3), CLUSTERS // CLDEV)
    col_device = jax.vmap(lambda own, number: shared_out(jax.random.fold_in(key_of[4], 2), own, number, CLDEV, N_CLU, NEAR, CAP, 1))(col_device_keys, col_device_turns).reshape((CLUSTERS, NEAR))
    col_local = touch_ends(jax.random.randint(key_of[5], (CLUSTERS, NEAR), 0, CLDEV), jax.random.fold_in(key_of[5], 1), 0, CLDEV - 1).astype(jnp.int32)
    ranks = touch_ends(jax.random.randint(key_of[6], (CLUSTERS,), SKEL // 2, SKEL + 1), jax.random.fold_in(key_of[6], 1), SKEL // 2, SKEL).astype(jnp.int32)
    parent_group_keys = jax.random.split(jax.random.fold_in(key_of[7], 1), CLUSTERS // CLDEV)
    parent_group_turns = jax.random.permutation(jax.random.fold_in(key_of[7], 3), CLUSTERS // CLDEV)
    parent_group = jax.vmap(lambda own, number: shared_out(jax.random.fold_in(key_of[7], 2), own, number, CLDEV, N_GRP, 1, MPG, 0))(parent_group_keys, parent_group_turns).reshape((CLUSTERS, 1))
    return {"near_blocks": near_blocks, "diag_blocks": diag_blocks, "bases": bases, "diag_inverses": diag_inverses, "col_device": col_device, "col_local": col_local, "ranks": ranks, "parent_group": parent_group}


HIGH = lax.Precision.HIGHEST


def prepare(basis, diagonal, inverse):
    redundant = BLOCK - SKEL
    left_product = jnp.dot(basis.T, diagonal, preferred_element_type=jnp.float32).astype(jnp.bfloat16)
    skel_red = jnp.dot(left_product[redundant:], basis[:, :redundant], preferred_element_type=jnp.float32)
    red_skel = jnp.dot(left_product[:redundant], basis[:, redundant:], preferred_element_type=jnp.float32)
    lower_factor = jnp.dot(skel_red, inverse, precision=HIGH)
    upper_factor = jnp.dot(inverse, red_skel, precision=HIGH)
    basis_wide = basis.astype(jnp.float32)
    row_basis = (basis_wide[:, redundant:].T - jnp.dot(lower_factor, basis_wide[:, :redundant].T, precision=HIGH)).astype(jnp.bfloat16)
    col_basis = (basis_wide[:, redundant:] - jnp.dot(basis_wide[:, :redundant], upper_factor, precision=HIGH)).astype(jnp.bfloat16)
    diag_left = jnp.dot(row_basis, diagonal, preferred_element_type=jnp.float32).astype(jnp.bfloat16)
    return row_basis, col_basis, diag_left


def rank_mask(row_ranks, col_ranks):
    skeleton_index = jnp.arange(SKEL, dtype=jnp.int32)
    rows_ok = skeleton_index[:, None] < row_ranks[..., None, None]
    cols_ok = skeleton_index[None, :] < col_ranks[..., None, None]
    return (rows_ok & cols_ok).astype(jnp.float32)


def running_slot(targets, buckets):
    onehot = (targets[..., None] == jnp.arange(buckets, dtype=jnp.int32)).astype(jnp.int32)
    before = jnp.cumsum(onehot, axis=-2) - onehot
    return jnp.sum(before * onehot, axis=-1).astype(jnp.int32)


def reference(near_blocks, diag_blocks, bases, diag_inverses, col_device, col_local, ranks, parent_group):
    def prepare_one(items):
        return prepare(items[0], items[1], items[2])

    row_basis, col_basis, diag_left = lax.map(prepare_one, (bases, diag_blocks, diag_inverses))

    def diag_reduce(items):
        product = jnp.dot(items[0], items[1], preferred_element_type=jnp.float32)
        return (product * rank_mask(items[2], items[2])).astype(jnp.bfloat16)

    rdiag = lax.map(diag_reduce, (diag_left, col_basis, ranks))

    cluster_ids = jnp.arange(CLUSTERS, dtype=jnp.int32)
    group_of = cluster_ids // (CLDEV * N_CLU)
    col_global = ((group_of[:, None] * N_CLU + col_device) * CLDEV + col_local).astype(jnp.int32)

    def near_reduce(items):
        blocks, row_one, columns, rank_one = items
        moved = jnp.einsum("sb,kbd->ksd", row_one.astype(jnp.float32), blocks.astype(jnp.float32)).astype(jnp.bfloat16)
        picked = col_basis[columns]
        product = jnp.einsum("ksd,kdt->kst", moved.astype(jnp.float32), picked.astype(jnp.float32))
        return (product * rank_mask(jnp.broadcast_to(rank_one, columns.shape), ranks[columns])).astype(jnp.bfloat16)

    reduced = lax.map(near_reduce, (near_blocks, row_basis, col_global, ranks))

    devices = N_GRP * N_CLU
    device_ids = jnp.arange(devices, dtype=jnp.int32)
    src_group = device_ids // N_CLU
    src_clu = device_ids % N_CLU
    destination = col_device.reshape(devices, CLDEV * NEAR)
    slot_index = running_slot(destination, N_CLU)
    flat_place = (((src_group[:, None] * N_CLU + destination) * N_CLU + src_clu[:, None]) * CAP + slot_index).astype(jnp.int32)
    reduced_near = jnp.zeros((devices * N_CLU * CAP, SKEL, SKEL), jnp.bfloat16)
    reduced_near = reduced_near.at[flat_place.reshape(-1)].set(reduced.reshape(-1, SKEL, SKEL))
    reduced_near = reduced_near.reshape(devices, N_CLU, CAP, SKEL, SKEL)

    parent_of = parent_group.reshape(devices, CLDEV)
    merge_slot = running_slot(parent_of, N_GRP)
    position = ((parent_of * N_CLU + src_clu[:, None]) * CLDEV + src_group[:, None] * MPG + merge_slot).astype(jnp.int32)
    merged = jnp.zeros((CLUSTERS, SKEL, SKEL), jnp.bfloat16).at[position.reshape(-1)].set(rdiag)
    merged = merged.reshape(PARENTS, 2, SKEL, SKEL)
    return reduced_near, merged
```

```python
import functools

import jax
import jax.numpy as jnp
from jax import lax
from jax.experimental import pallas as pl
from jax.experimental.pallas import tpu as pltpu
from jax.sharding import PartitionSpec as P

BF16 = jnp.bfloat16
F32 = jnp.float32
CAPACITY = 2


def dot(a, b):
    return jnp.dot(a, b, preferred_element_type=F32)


def dot_nt(a, b):
    return lax.dot_general(a, b, (((1,), (1,)), ((), ())), preferred_element_type=F32)


def halves(x):
    high = x.astype(BF16)
    return high, (x - high.astype(F32)).astype(BF16)


def dot_wide(a, b):
    a_high, a_low = halves(a)
    b_high, b_low = halves(b)
    upper = jnp.concatenate([b_high, b_low], 1)
    lower = jnp.concatenate([b_high, jnp.zeros_like(b_low)], 1)
    both = dot(jnp.concatenate([a_high, a_low], 1), jnp.concatenate([upper, lower], 0))
    return both[:, : b.shape[1]] + both[:, b.shape[1] :]


def move_kernel(
    near_count,
    group,
    col_device_hbm,
    col_local_hbm,
    ranks_hbm,
    bases_hbm,
    diag_hbm,
    inverse_hbm,
    near_hbm,
    send_hbm,
    row_hbm,
    meta_hbm,
    col_device,
    col_local,
    ranks,
    bases,
    diag,
    inverse,
    near,
    rows,
    moved,
    count,
    place,
    meta,
    int_sem,
    in_sem,
    near_sem,
    out_sem,
    row_sem,
):
    local_count, block, _ = bases.shape
    redundant = inverse.shape[1]
    skeleton = block - redundant
    groups = local_count // group
    ints = (
        pltpu.make_async_copy(col_device_hbm, col_device, int_sem.at[0]),
        pltpu.make_async_copy(col_local_hbm, col_local, int_sem.at[1]),
        pltpu.make_async_copy(ranks_hbm, ranks, int_sem.at[2]),
    )
    meta_copy = pltpu.make_async_copy(meta, meta_hbm, int_sem.at[3])

    def inputs(g):
        part = pl.ds(g * group, group)
        return (
            pltpu.make_async_copy(bases_hbm.at[part], bases.at[part], in_sem.at[g, 0]),
            pltpu.make_async_copy(diag_hbm.at[part], diag.at[part], in_sem.at[g, 1]),
            pltpu.make_async_copy(inverse_hbm.at[part], inverse.at[part], in_sem.at[g, 2]),
        )

    def near_copy(c):
        return pltpu.make_async_copy(near_hbm.at[c], near.at[c], near_sem.at[c])

    def out_copy(c, k):
        return pltpu.make_async_copy(moved.at[c, k], send_hbm.at[place[c, k]], out_sem.at[c, k])

    def row_copy(g):
        part = pl.ds(g * group, group)
        return pltpu.make_async_copy(rows.at[part], row_hbm.at[part], row_sem.at[g])

    for copy in ints:
        copy.start()
    for g in range(groups):
        for copy in inputs(g):
            copy.start()
        for c in range(g * group, (g + 1) * group):
            near_copy(c).start()

    def clear(d, carry):
        count[d] = 0
        for s in range(CAPACITY):
            meta[d, s] = -1
        return carry

    lax.fori_loop(0, count.shape[0], clear, 0)
    for copy in ints:
        copy.wait()

    def assign(l, carry):
        for k in range(near_count):
            d = col_device[l, k]
            s = count[d]
            count[d] = s + 1
            meta[d, s] = col_local[l, k]
            place[l, k] = d * CAPACITY + s
        return carry

    lax.fori_loop(0, local_count, assign, 0)
    meta_copy.start()

    def prepare(members):
        red = [bases[c][:, :redundant] for c in members]
        skel_t = [bases[c][:, redundant:].T for c in members]
        left = [dot(s, diag[c]).astype(BF16) for s, c in zip(skel_t, members)]
        factor = [dot(l, r) for l, r in zip(left, red)]
        lower = [halves(dot_wide(f, inverse[c])) for f, c in zip(factor, members)]
        taken = [
            dot_nt(jnp.concatenate(pair, 1), jnp.concatenate([r, r], 1))
            for pair, r in zip(lower, red)
        ]
        for c, s, t in zip(members, skel_t, taken):
            rows[c] = (s.astype(F32) - t).astype(BF16)

    rows_at = lax.broadcasted_iota(jnp.int32, (skeleton, block), 0)

    def step(c, carry):
        near_copy(c).wait()
        keep = rows_at < ranks[c]
        row = rows[c]
        for k in range(near_count):
            moved[c, k] = jnp.where(keep, dot(row, near[c, k]), 0.0).astype(BF16)
        for k in range(near_count):
            out_copy(c, k).start()
        return carry

    for g in range(groups):
        for copy in inputs(g):
            copy.wait()
        prepare(range(g * group, (g + 1) * group))
        row_copy(g).start()
        lax.fori_loop(g * group, (g + 1) * group, step, 0)

    for g in range(groups):
        row_copy(g).wait()
    meta_copy.wait()

    def finish(c, carry):
        for k in range(near_count):
            out_copy(c, k).wait()
        return carry

    lax.fori_loop(0, local_count, finish, 0)


def move_blocks(near_blocks, diag_blocks, bases, diag_inverses, col_device, col_local, ranks, buckets):
    local_count, near_count, block, _ = near_blocks.shape
    redundant = diag_inverses.shape[1]
    skeleton = block - redundant
    group = 4
    groups = local_count // group
    hbm = pl.BlockSpec(memory_space=pl.ANY)
    dma = pltpu.SemaphoreType.DMA
    return pl.pallas_call(
        functools.partial(move_kernel, near_count, group),
        out_shape=(
            jax.ShapeDtypeStruct((buckets * CAPACITY, skeleton, block), BF16),
            jax.ShapeDtypeStruct((local_count, skeleton, block), BF16),
            jax.ShapeDtypeStruct((buckets, CAPACITY), jnp.int32),
        ),
        in_specs=[hbm] * 7,
        out_specs=(hbm, hbm, hbm),
        scratch_shapes=[
            pltpu.SMEM((local_count, near_count), jnp.int32),
            pltpu.SMEM((local_count, near_count), jnp.int32),
            pltpu.SMEM((local_count,), jnp.int32),
            pltpu.VMEM((local_count, block, block), BF16),
            pltpu.VMEM((local_count, block, block), BF16),
            pltpu.VMEM((local_count, redundant, redundant), F32),
            pltpu.VMEM((local_count, near_count, block, block), BF16),
            pltpu.VMEM((local_count, skeleton, block), BF16),
            pltpu.VMEM((local_count, near_count, skeleton, block), BF16),
            pltpu.SMEM((buckets,), jnp.int32),
            pltpu.SMEM((local_count, near_count), jnp.int32),
            pltpu.SMEM((buckets, CAPACITY), jnp.int32),
            dma((4,)),
            dma((groups, 3)),
            dma((local_count,)),
            dma((local_count, near_count)),
            dma((groups,)),
        ],
        compiler_params=pltpu.CompilerParams(vmem_limit_bytes=56 * 2**20),
        cost_estimate=pl.CostEstimate(
            flops=2 * 10**9, bytes_accessed=13 * 10**6, transcendentals=0
        ),
        name="move_blocks",
    )(col_device, col_local, ranks, bases, diag_blocks, diag_inverses, near_blocks)


def diagonal_kernel(parent, ranks, basis_ref, diag_ref, inverse_ref, row_ref, out_ref, col_ref):
    c = pl.program_id(0)
    redundant = inverse_ref.shape[1]
    basis = basis_ref[0]
    diagonal = diag_ref[0]
    red = basis[:, :redundant]
    skel = basis[:, redundant:]
    left = dot(red.T, diagonal).astype(BF16)
    upper = dot_wide(inverse_ref[0], dot(left, skel))
    high, low = halves(upper)
    col = (skel.astype(F32) - (dot(red, high) + dot(red, low))).astype(BF16)
    col_ref[0] = col
    reduced = dot(dot(row_ref[0], diagonal).astype(BF16), col)
    rank = ranks[c]
    rows_at = lax.broadcasted_iota(jnp.int32, reduced.shape, 0)
    cols_at = lax.broadcasted_iota(jnp.int32, reduced.shape, 1)
    keep = (rows_at < rank) & (cols_at < rank)
    out_ref[0] = jnp.where(keep, reduced, 0.0).astype(BF16)


def diagonal_part(bases, diag_blocks, diag_inverses, row_basis, ranks, parent_group):
    local_count, block, _ = bases.shape
    redundant = diag_inverses.shape[1]
    skeleton = block - redundant

    def own(*shape):
        return pl.BlockSpec((1,) + shape, lambda c, parent, ranks: (c, 0, 0))

    return pl.pallas_call(
        diagonal_kernel,
        out_shape=(
            jax.ShapeDtypeStruct((local_count, skeleton, skeleton), BF16),
            jax.ShapeDtypeStruct((local_count, block, skeleton), BF16),
        ),
        grid_spec=pltpu.PrefetchScalarGridSpec(
            num_scalar_prefetch=2,
            grid=(local_count,),
            in_specs=[
                own(block, block),
                own(block, block),
                own(redundant, redundant),
                own(skeleton, block),
            ],
            out_specs=[
                pl.BlockSpec(
                    (1, skeleton, skeleton), lambda c, parent, ranks: (parent[c], 0, 0)
                ),
                own(block, skeleton),
            ],
        ),
        compiler_params=pltpu.CompilerParams(vmem_limit_bytes=16 * 2**20),
        cost_estimate=pl.CostEstimate(
            flops=10**9, bytes_accessed=4 * 10**6, transcendentals=0
        ),
        name="diagonal_part",
    )(parent_group[:, 0], ranks, bases, diag_blocks, diag_inverses, row_basis)


def reduce_kernel(
    chunk,
    meta_hbm,
    ranks_hbm,
    moved_hbm,
    col_hbm,
    out_hbm,
    meta,
    ranks,
    moved,
    col,
    out,
    int_sem,
    in_sem,
    out_sem,
):
    steps = moved.shape[0] // chunk
    firsts = (
        pltpu.make_async_copy(meta_hbm, meta, int_sem.at[0]),
        pltpu.make_async_copy(ranks_hbm, ranks, int_sem.at[1]),
        pltpu.make_async_copy(col_hbm, col, int_sem.at[2]),
    )

    def in_copy(i):
        part = pl.ds(i * chunk, chunk)
        return pltpu.make_async_copy(moved_hbm.at[part], moved.at[part], in_sem.at[i])

    def out_copy(i):
        part = pl.ds(i * chunk, chunk)
        return pltpu.make_async_copy(out.at[part], out_hbm.at[part], out_sem.at[i])

    for copy in firsts:
        copy.start()
    for i in range(steps):
        in_copy(i).start()
    for copy in firsts:
        copy.wait()
    cols_at = lax.broadcasted_iota(jnp.int32, out.shape[1:], 1)

    def step(i, carry):
        in_copy(i).wait()
        for j in range(chunk):
            e = i * chunk + j
            local = meta[i * (chunk // CAPACITY) + j // CAPACITY, j % CAPACITY]
            owner = jnp.maximum(local, 0)
            rank = jnp.where(local < 0, 0, ranks[owner])
            out[e] = jnp.where(cols_at < rank, dot(moved[e], col[owner]), 0.0).astype(BF16)
        out_copy(i).start()
        return carry

    lax.fori_loop(0, steps, step, 0)
    for i in range(steps):
        out_copy(i).wait()


def reduce_blocks(moved, meta, col_basis, ranks):
    slots, skeleton, block = moved.shape
    chunk = 16
    hbm = pl.BlockSpec(memory_space=pl.ANY)
    dma = pltpu.SemaphoreType.DMA
    return pl.pallas_call(
        functools.partial(reduce_kernel, chunk),
        out_shape=jax.ShapeDtypeStruct((slots, skeleton, skeleton), BF16),
        in_specs=[hbm] * 4,
        out_specs=hbm,
        scratch_shapes=[
            pltpu.SMEM(meta.shape, jnp.int32),
            pltpu.SMEM(ranks.shape, jnp.int32),
            pltpu.VMEM(moved.shape, BF16),
            pltpu.VMEM(col_basis.shape, BF16),
            pltpu.VMEM((slots, skeleton, skeleton), BF16),
            dma((3,)),
            dma((slots // chunk,)),
            dma((slots // chunk,)),
        ],
        compiler_params=pltpu.CompilerParams(vmem_limit_bytes=56 * 2**20),
        cost_estimate=pl.CostEstimate(
            flops=6 * 10**8, bytes_accessed=7 * 10**6, transcendentals=0
        ),
        name="reduce_blocks",
    )(meta, ranks, moved, col_basis)


def swap_halves(x, axis_name):
    size = lax.axis_size(axis_name)
    me = lax.axis_index(axis_name)
    bit = 1
    while bit < size:
        pairs = x.reshape((size // (2 * bit), 2, bit) + x.shape[1:])
        mine = (me // bit) % 2
        kept = lax.dynamic_index_in_dim(pairs, mine, 1, keepdims=False)
        given = lax.dynamic_index_in_dim(pairs, 1 - mine, 1, keepdims=False)
        got = lax.ppermute(given, axis_name, [(i, i ^ bit) for i in range(size)])
        low, high = jnp.stack([kept, got], 1), jnp.stack([got, kept], 1)
        x = jnp.where(mine == 0, low, high).reshape(x.shape)
        bit *= 2
    return x


def on_device(
    near_blocks, diag_blocks, bases, diag_inverses, col_device, col_local, ranks, parent_group
):
    buckets = lax.axis_size("clu")
    local_count = ranks.shape[0]
    send, row_basis, meta = move_blocks(
        near_blocks, diag_blocks, bases, diag_inverses, col_device, col_local, ranks, buckets
    )
    skeleton, block = send.shape[1:]
    received = lax.all_to_all(
        send.reshape(buckets, CAPACITY, skeleton, block), "clu", 0, 0, tiled=True
    )
    came_meta = swap_halves(meta, "clu")
    outgoing, col_basis = diagonal_part(
        bases, diag_blocks, diag_inverses, row_basis, ranks, parent_group
    )
    arrived = swap_halves(outgoing, "grp")
    merged = arrived.reshape(local_count // 2, 2, skeleton, skeleton)
    reduced = reduce_blocks(
        received.reshape(buckets * CAPACITY, skeleton, block), came_meta, col_basis, ranks
    )
    return reduced.reshape(1, buckets, CAPACITY, skeleton, skeleton), merged


def solution(mesh):
    in_specs = (
        P(("grp", "clu"), None, None, None),
        P(("grp", "clu"), None, None),
        P(("grp", "clu"), None, None),
        P(("grp", "clu"), None, None),
        P(("grp", "clu"), None),
        P(("grp", "clu"), None),
        P(("grp", "clu")),
        P(("grp", "clu"), None),
    )
    out_specs = (P(("grp", "clu"), None, None, None, None), P(("grp", "clu"), None, None, None))
    return jax.shard_map(
        on_device, mesh=mesh, in_specs=in_specs, out_specs=out_specs, check_vma=False
    )
```

```python
import functools

import jax
import jax.numpy as jnp
from jax import lax
from jax.experimental import pallas as pl
from jax.experimental.pallas import tpu as pltpu
from jax.sharding import PartitionSpec as P

BF16 = jnp.bfloat16
F32 = jnp.float32
CAPACITY = 2
NOTE_ROWS = 16


def dot(a, b):
    return jnp.dot(a, b, preferred_element_type=F32)


def dot_nt(a, b):
    return lax.dot_general(a, b, (((1,), (1,)), ((), ())), preferred_element_type=F32)


def halves(x):
    high = x.astype(BF16)
    return high, (x - high.astype(F32)).astype(BF16)


def dot_wide(a, b):
    a_high, a_low = halves(a)
    b_high, b_low = halves(b)
    upper = jnp.concatenate([b_high, b_low], 1)
    lower = jnp.concatenate([b_high, jnp.zeros_like(b_low)], 1)
    both = dot(jnp.concatenate([a_high, a_low], 1), jnp.concatenate([upper, lower], 0))
    return both[:, : b.shape[1]] + both[:, b.shape[1] :]


def move_kernel(
    near_count,
    groups,
    targets_hbm,
    locals_hbm,
    ranks_hbm,
    bases_hbm,
    diag_hbm,
    inverse_hbm,
    near_hbm,
    send_hbm,
    row_hbm,
    targets,
    locals_,
    ranks,
    bases,
    diag,
    inverse,
    near,
    rows,
    moved,
    notes,
    count,
    place,
    codes,
    int_sem,
    in_sem,
    near_sem,
    out_sem,
    row_sem,
):
    local_count, block, _ = bases.shape
    redundant = inverse.shape[1]
    skeleton = block - redundant
    members = []
    for size in groups:
        first = members[-1][-1] + 1 if members else 0
        members.append(range(first, first + size))
    ints = (
        pltpu.make_async_copy(targets_hbm, targets, int_sem.at[0]),
        pltpu.make_async_copy(ranks_hbm, ranks, int_sem.at[1]),
        pltpu.make_async_copy(locals_hbm, locals_, int_sem.at[2]),
    )
    body = CAPACITY * 2 * skeleton
    note_copy = pltpu.make_async_copy(
        notes, send_hbm.at[:, pl.ds(body, NOTE_ROWS)], row_sem.at[1]
    )
    row_copy = pltpu.make_async_copy(rows, row_hbm, row_sem.at[0])

    def part(g):
        return pl.ds(members[g][0], len(members[g]))

    def inputs(g):
        return (
            pltpu.make_async_copy(bases_hbm.at[part(g)], bases.at[part(g)], in_sem.at[g, 0]),
            pltpu.make_async_copy(diag_hbm.at[part(g)], diag.at[part(g)], in_sem.at[g, 1]),
            pltpu.make_async_copy(inverse_hbm.at[part(g)], inverse.at[part(g)], in_sem.at[g, 2]),
        )

    def near_copy(g):
        return pltpu.make_async_copy(near_hbm.at[part(g)], near.at[part(g)], near_sem.at[g])

    def out_copy(c, k):
        row = pl.multiple_of(place[c, k] * 2 * skeleton, 2 * skeleton)
        target = send_hbm.at[targets[c, k], pl.ds(row, 2 * skeleton)]
        return pltpu.make_async_copy(moved.at[c, k], target, out_sem.at[c, k])

    for g in range(len(groups)):
        for copy in inputs(g):
            copy.start()
        if g == 0:
            for copy in ints:
                copy.start()
        near_copy(g).start()

    def clear(d, carry):
        count[d] = 0
        for s in range(CAPACITY):
            codes[d, s] = -1
        return carry

    lax.fori_loop(0, count.shape[0], clear, 0)
    for copy in ints:
        copy.wait()

    def assign(l, carry):
        for k in range(near_count):
            d = targets[l, k]
            s = count[d]
            place[l, k] = s
            count[d] = s + 1
            codes[d, s] = locals_[l, k]
        return carry

    lax.fori_loop(0, local_count, assign, 0)

    lanes = lax.broadcasted_iota(jnp.int32, notes.shape[1:], 1)

    def write_note(d, carry):
        note = jnp.full(notes.shape[1:], -1, jnp.int32)
        for s in range(CAPACITY):
            note = jnp.where(lanes == s, codes[d, s], note)
        notes[d] = note.astype(F32).astype(BF16)
        return carry

    lax.fori_loop(0, count.shape[0], write_note, 0)
    note_copy.start()

    def prepare(g):
        red = [bases[c][:, :redundant] for c in members[g]]
        skel_t = [bases[c][:, redundant:].T for c in members[g]]
        left = [dot(s, diag[c]).astype(BF16) for s, c in zip(skel_t, members[g])]
        factor = [dot(l, r) for l, r in zip(left, red)]
        lower = [halves(dot_wide(f, inverse[c])) for f, c in zip(factor, members[g])]
        taken = [
            dot_nt(jnp.concatenate(pair, 1), jnp.concatenate([r, r], 1))
            for pair, r in zip(lower, red)
        ]
        for c, s, t in zip(members[g], skel_t, taken):
            rows[c] = (s.astype(F32) - t).astype(BF16)

    rows_at = lax.broadcasted_iota(jnp.int32, (skeleton, block), 0)

    def move(g):
        for c in members[g]:
            keep = rows_at < ranks[c]
            row = rows[c]
            for k in range(near_count):
                product = jnp.where(keep, dot(row, near[c, k]), 0.0).astype(BF16)
                moved[c, k, :skeleton] = product[:, :skeleton]
                moved[c, k, skeleton:] = product[:, skeleton:]

    def send_one(c, carry):
        for k in range(near_count):
            out_copy(c, k).start()
        return carry

    def finish_one(c, carry):
        for k in range(near_count):
            out_copy(c, k).wait()
        return carry

    for copy in inputs(0):
        copy.wait()
    prepare(0)
    for g in range(len(groups)):
        near_copy(g).wait()
        if g + 1 < len(groups):
            for copy in inputs(g + 1):
                copy.wait()
        move(g)
        if g + 1 < len(groups):
            prepare(g + 1)
        lax.fori_loop(members[g][0], members[g][-1] + 1, send_one, 0)
        if g + 2 == len(groups):
            row_copy.start()
    row_copy.wait()
    note_copy.wait()
    lax.fori_loop(0, local_count, finish_one, 0)


def move_blocks(near_blocks, diag_blocks, bases, diag_inverses, col_device, col_local, ranks, buckets):
    local_count, near_count, block, _ = near_blocks.shape
    redundant = diag_inverses.shape[1]
    skeleton = block - redundant
    groups = (2, 3, 3)
    hbm = pl.BlockSpec(memory_space=pl.ANY)
    dma = pltpu.SemaphoreType.DMA
    return pl.pallas_call(
        functools.partial(move_kernel, near_count, groups),
        out_shape=(
            jax.ShapeDtypeStruct((buckets, CAPACITY * block + NOTE_ROWS, skeleton), BF16),
            jax.ShapeDtypeStruct((local_count, skeleton, block), BF16),
        ),
        in_specs=[hbm] * 7,
        out_specs=(hbm, hbm),
        scratch_shapes=[
            pltpu.SMEM((local_count, near_count), jnp.int32),
            pltpu.SMEM((local_count, near_count), jnp.int32),
            pltpu.SMEM((local_count,), jnp.int32),
            pltpu.VMEM((local_count, block, block), BF16),
            pltpu.VMEM((local_count, block, block), BF16),
            pltpu.VMEM((local_count, redundant, redundant), F32),
            pltpu.VMEM((local_count, near_count, block, block), BF16),
            pltpu.VMEM((local_count, skeleton, block), BF16),
            pltpu.VMEM((local_count, near_count, 2 * skeleton, skeleton), BF16),
            pltpu.VMEM((buckets, NOTE_ROWS, skeleton), BF16),
            pltpu.SMEM((buckets,), jnp.int32),
            pltpu.SMEM((local_count, near_count), jnp.int32),
            pltpu.SMEM((buckets, CAPACITY), jnp.int32),
            dma((3,)),
            dma((len(groups), 3)),
            dma((len(groups),)),
            dma((local_count, near_count)),
            dma((2,)),
        ],
        compiler_params=pltpu.CompilerParams(vmem_limit_bytes=56 * 2**20),
        cost_estimate=pl.CostEstimate(
            flops=2 * 10**9, bytes_accessed=13 * 10**6, transcendentals=0
        ),
        name="move_blocks",
    )(col_device, col_local, ranks, bases, diag_blocks, diag_inverses, near_blocks)


def diagonal_kernel(parent, ranks, basis_ref, diag_ref, inverse_ref, row_ref, out_ref, col_ref):
    c = pl.program_id(0)
    redundant = inverse_ref.shape[1]
    basis = basis_ref[0]
    diagonal = diag_ref[0]
    red = basis[:, :redundant]
    skel = basis[:, redundant:]
    left = dot(red.T, diagonal).astype(BF16)
    upper = dot_wide(inverse_ref[0], dot(left, skel))
    high, low = halves(upper)
    col = (skel.astype(F32) - (dot(red, high) + dot(red, low))).astype(BF16)
    col_ref[0] = col
    reduced = dot(dot(row_ref[0], diagonal).astype(BF16), col)
    rank = ranks[c]
    rows_at = lax.broadcasted_iota(jnp.int32, reduced.shape, 0)
    cols_at = lax.broadcasted_iota(jnp.int32, reduced.shape, 1)
    keep = (rows_at < rank) & (cols_at < rank)
    out_ref[0] = jnp.where(keep, reduced, 0.0).astype(BF16)


def diagonal_part(bases, diag_blocks, diag_inverses, row_basis, ranks, parent_group):
    local_count, block, _ = bases.shape
    redundant = diag_inverses.shape[1]
    skeleton = block - redundant

    def own(*shape):
        return pl.BlockSpec((1,) + shape, lambda c, parent, ranks: (c, 0, 0))

    return pl.pallas_call(
        diagonal_kernel,
        out_shape=(
            jax.ShapeDtypeStruct((local_count, skeleton, skeleton), BF16),
            jax.ShapeDtypeStruct((local_count, block, skeleton), BF16),
        ),
        grid_spec=pltpu.PrefetchScalarGridSpec(
            num_scalar_prefetch=2,
            grid=(local_count,),
            in_specs=[
                own(block, block),
                own(block, block),
                own(redundant, redundant),
                own(skeleton, block),
            ],
            out_specs=[
                pl.BlockSpec(
                    (1, skeleton, skeleton), lambda c, parent, ranks: (parent[c], 0, 0)
                ),
                own(block, skeleton),
            ],
        ),
        compiler_params=pltpu.CompilerParams(vmem_limit_bytes=16 * 2**20),
        cost_estimate=pl.CostEstimate(
            flops=10**9, bytes_accessed=4 * 10**6, transcendentals=0
        ),
        name="diagonal_part",
    )(parent_group[:, 0], ranks, bases, diag_blocks, diag_inverses, row_basis)


def reduce_kernel(
    chunk,
    ranks_hbm,
    came_hbm,
    col_hbm,
    out_hbm,
    ranks,
    came,
    notes,
    local_rows,
    locals_,
    col,
    out,
    first_sem,
    in_sem,
    out_sem,
):
    sources = came.shape[0]
    skeleton = came.shape[2]
    body = came.shape[1]
    steps = sources // chunk
    ranks_copy = pltpu.make_async_copy(ranks_hbm, ranks, first_sem.at[0])
    col_copy = pltpu.make_async_copy(col_hbm, col, first_sem.at[1])
    note_copy = pltpu.make_async_copy(
        came_hbm.at[:, pl.ds(body, NOTE_ROWS)], notes, first_sem.at[2]
    )
    local_copy = pltpu.make_async_copy(local_rows, locals_, first_sem.at[3])

    def in_copy(i):
        part = pl.ds(i * chunk, chunk)
        return pltpu.make_async_copy(
            came_hbm.at[part, pl.ds(0, body)], came.at[part], in_sem.at[i]
        )

    def out_copy(i):
        part = pl.ds(i * chunk * CAPACITY, chunk * CAPACITY)
        return pltpu.make_async_copy(out.at[part], out_hbm.at[part], out_sem.at[i])

    note_copy.start()
    ranks_copy.start()
    col_copy.start()
    for i in range(steps):
        in_copy(i).start()
    note_copy.wait()
    local_rows[...] = notes[:, 0, :].astype(F32).astype(jnp.int32)
    local_copy.start()
    ranks_copy.wait()
    col_copy.wait()
    local_copy.wait()
    cols_at = lax.broadcasted_iota(jnp.int32, out.shape[1:], 1)

    def step(i, carry):
        in_copy(i).wait()
        for j in range(chunk):
            source = i * chunk + j
            for s in range(CAPACITY):
                local = locals_[source, s]
                owner = jnp.maximum(local, 0)
                rank = jnp.where(local < 0, 0, ranks[owner])
                top = 2 * s * skeleton
                moved = jnp.concatenate(
                    [came[source, pl.ds(top, skeleton)], came[source, pl.ds(top + skeleton, skeleton)]],
                    1,
                )
                product = dot(moved, col[owner])
                out[source * CAPACITY + s] = jnp.where(cols_at < rank, product, 0.0).astype(BF16)
        out_copy(i).start()
        return carry

    lax.fori_loop(0, steps, step, 0)
    for i in range(steps):
        out_copy(i).wait()


def reduce_blocks(received, col_basis, ranks):
    sources, rows, skeleton = received.shape
    body = rows - NOTE_ROWS
    chunk = 16
    hbm = pl.BlockSpec(memory_space=pl.ANY)
    dma = pltpu.SemaphoreType.DMA
    return pl.pallas_call(
        functools.partial(reduce_kernel, chunk),
        out_shape=jax.ShapeDtypeStruct((sources * CAPACITY, skeleton, skeleton), BF16),
        in_specs=[hbm] * 3,
        out_specs=hbm,
        scratch_shapes=[
            pltpu.SMEM(ranks.shape, jnp.int32),
            pltpu.VMEM((sources, body, skeleton), BF16),
            pltpu.VMEM((sources, NOTE_ROWS, skeleton), BF16),
            pltpu.VMEM((sources, skeleton), jnp.int32),
            pltpu.SMEM((sources, skeleton), jnp.int32),
            pltpu.VMEM(col_basis.shape, BF16),
            pltpu.VMEM((sources * CAPACITY, skeleton, skeleton), BF16),
            dma((4,)),
            dma((sources // chunk,)),
            dma((sources // chunk,)),
        ],
        compiler_params=pltpu.CompilerParams(vmem_limit_bytes=56 * 2**20),
        cost_estimate=pl.CostEstimate(
            flops=6 * 10**8, bytes_accessed=7 * 10**6, transcendentals=0
        ),
        name="reduce_blocks",
    )(ranks, received, col_basis)


def swap_halves(x, axis_name):
    size = lax.axis_size(axis_name)
    me = lax.axis_index(axis_name)
    bit = 1
    while bit < size:
        pairs = x.reshape((size // (2 * bit), 2, bit) + x.shape[1:])
        mine = (me // bit) % 2
        kept = lax.dynamic_index_in_dim(pairs, mine, 1, keepdims=False)
        given = lax.dynamic_index_in_dim(pairs, 1 - mine, 1, keepdims=False)
        got = lax.ppermute(given, axis_name, [(i, i ^ bit) for i in range(size)])
        low, high = jnp.stack([kept, got], 1), jnp.stack([got, kept], 1)
        x = jnp.where(mine == 0, low, high).reshape(x.shape)
        bit *= 2
    return x


def on_device(
    near_blocks, diag_blocks, bases, diag_inverses, col_device, col_local, ranks, parent_group
):
    buckets = lax.axis_size("clu")
    local_count = ranks.shape[0]
    send, row_basis = move_blocks(
        near_blocks, diag_blocks, bases, diag_inverses, col_device, col_local, ranks, buckets
    )
    skeleton = send.shape[2]
    received = lax.all_to_all(send, "clu", 0, 0, tiled=True)
    outgoing, col_basis = diagonal_part(
        bases, diag_blocks, diag_inverses, row_basis, ranks, parent_group
    )
    merged = swap_halves(outgoing, "grp").reshape(local_count // 2, 2, skeleton, skeleton)
    reduced = reduce_blocks(received, col_basis, ranks)
    return reduced.reshape(1, buckets, CAPACITY, skeleton, skeleton), merged


def solution(mesh):
    in_specs = (
        P(("grp", "clu"), None, None, None),
        P(("grp", "clu"), None, None),
        P(("grp", "clu"), None, None),
        P(("grp", "clu"), None, None),
        P(("grp", "clu"), None),
        P(("grp", "clu"), None),
        P(("grp", "clu")),
        P(("grp", "clu"), None),
    )
    out_specs = (P(("grp", "clu"), None, None, None, None), P(("grp", "clu"), None, None, None))
    return jax.shard_map(
        on_device, mesh=mesh, in_specs=in_specs, out_specs=out_specs, check_vma=False
    )
```

```python
import functools

import jax
import jax.numpy as jnp
from jax import lax
from jax.experimental import pallas as pl
from jax.experimental.pallas import tpu as pltpu
from jax.sharding import PartitionSpec as P

BF16 = jnp.bfloat16
F32 = jnp.float32
CAPACITY = 2
NOTE_ROWS = 8
GROUPS = (2, 4, 2)
CHUNKS = (16, 16)


def dot(a, b):
    return jnp.dot(a, b, preferred_element_type=F32)


def dot_nt(a, b):
    return lax.dot_general(a, b, (((1,), (1,)), ((), ())), preferred_element_type=F32)


def halves(x):
    high = x.astype(BF16)
    return high, (x - high.astype(F32)).astype(BF16)


def dot_wide(a, b):
    a_high, a_low = halves(a)
    b_high, b_low = halves(b)
    upper = jnp.concatenate([b_high, b_low], 1)
    lower = jnp.concatenate([b_high, jnp.zeros_like(b_low)], 1)
    both = dot(jnp.concatenate([a_high, a_low], 1), jnp.concatenate([upper, lower], 0))
    return both[:, : b.shape[1]] + both[:, b.shape[1] :]


def move_kernel(
    near_count,
    groups,
    targets_hbm,
    locals_hbm,
    ranks_hbm,
    bases_hbm,
    diag_hbm,
    inverse_hbm,
    near_hbm,
    send_hbm,
    targets,
    locals_,
    ranks,
    bases,
    diag,
    inverse,
    near,
    rows,
    moved,
    notes,
    count,
    place,
    codes,
    int_sem,
    in_sem,
    near_sem,
    out_sem,
    note_sem,
):
    local_count, block, _ = bases.shape
    redundant = inverse.shape[1]
    skeleton = block - redundant
    members = []
    for size in groups:
        first = members[-1][-1] + 1 if members else 0
        members.append(range(first, first + size))
    ints = (
        pltpu.make_async_copy(targets_hbm, targets, int_sem.at[0]),
        pltpu.make_async_copy(ranks_hbm, ranks, int_sem.at[1]),
        pltpu.make_async_copy(locals_hbm, locals_, int_sem.at[2]),
    )
    body = CAPACITY * 2 * skeleton
    note_copy = pltpu.make_async_copy(
        notes, send_hbm.at[:, pl.ds(body, NOTE_ROWS)], note_sem.at[0]
    )

    def part(g):
        return pl.ds(members[g][0], len(members[g]))

    def inputs(g):
        return (
            pltpu.make_async_copy(bases_hbm.at[part(g)], bases.at[part(g)], in_sem.at[g, 0]),
            pltpu.make_async_copy(diag_hbm.at[part(g)], diag.at[part(g)], in_sem.at[g, 1]),
            pltpu.make_async_copy(inverse_hbm.at[part(g)], inverse.at[part(g)], in_sem.at[g, 2]),
        )

    def near_copy(g):
        return pltpu.make_async_copy(near_hbm.at[part(g)], near.at[part(g)], near_sem.at[g])

    def out_copy(c, k):
        row = pl.multiple_of(place[c, k] * 2 * skeleton, 2 * skeleton)
        target = send_hbm.at[targets[c, k], pl.ds(row, 2 * skeleton)]
        return pltpu.make_async_copy(moved.at[c, k], target, out_sem.at[c, k])

    for g in range(len(groups)):
        for copy in inputs(g):
            copy.start()
        if g == 0:
            for copy in ints:
                copy.start()
        near_copy(g).start()

    def clear(d, carry):
        count[d] = 0
        for s in range(CAPACITY):
            codes[d, s] = -1
        return carry

    lax.fori_loop(0, count.shape[0], clear, 0)
    for copy in ints:
        copy.wait()

    def assign(l, carry):
        for k in range(near_count):
            d = targets[l, k]
            s = count[d]
            place[l, k] = s
            count[d] = s + 1
            codes[d, s] = locals_[l, k]
        return carry

    lax.fori_loop(0, local_count, assign, 0)

    lanes = lax.broadcasted_iota(jnp.int32, notes.shape[1:], 1)

    def write_note(d, carry):
        note = jnp.full(notes.shape[1:], -1, jnp.int32)
        for s in range(CAPACITY):
            note = jnp.where(lanes == s, codes[d, s], note)
        notes[d] = note.astype(F32).astype(BF16)
        return carry

    lax.fori_loop(0, count.shape[0], write_note, 0)
    note_copy.start()

    def prepare(g):
        red = [bases[c][:, :redundant] for c in members[g]]
        skel_t = [bases[c][:, redundant:].T for c in members[g]]
        left = [dot(s, diag[c]).astype(BF16) for s, c in zip(skel_t, members[g])]
        factor = [dot(l, r) for l, r in zip(left, red)]
        lower = [halves(dot_wide(f, inverse[c])) for f, c in zip(factor, members[g])]
        taken = [
            dot_nt(jnp.concatenate(pair, 1), jnp.concatenate([r, r], 1))
            for pair, r in zip(lower, red)
        ]
        for c, s, t in zip(members[g], skel_t, taken):
            rows[c] = (s.astype(F32) - t).astype(BF16)

    rows_at = lax.broadcasted_iota(jnp.int32, (skeleton, block), 0)

    def move(g):
        for c in members[g]:
            keep = rows_at < ranks[c]
            row = rows[c]
            for k in range(near_count):
                product = jnp.where(keep, dot(row, near[c, k]), 0.0).astype(BF16)
                moved[c, k, :skeleton] = product[:, :skeleton]
                moved[c, k, skeleton:] = product[:, skeleton:]

    def send_one(c, carry):
        for k in range(near_count):
            out_copy(c, k).start()
        return carry

    def finish_one(c, carry):
        for k in range(near_count):
            out_copy(c, k).wait()
        return carry

    for copy in inputs(0):
        copy.wait()
    prepare(0)
    for g in range(len(groups)):
        near_copy(g).wait()
        if g + 1 < len(groups):
            for copy in inputs(g + 1):
                copy.wait()
        move(g)
        if g + 1 < len(groups):
            prepare(g + 1)
        lax.fori_loop(members[g][0], members[g][-1] + 1, send_one, 0)
    note_copy.wait()
    lax.fori_loop(0, local_count, finish_one, 0)


def move_blocks(near_blocks, diag_blocks, bases, diag_inverses, col_device, col_local, ranks, buckets):
    local_count, near_count, block, _ = near_blocks.shape
    redundant = diag_inverses.shape[1]
    skeleton = block - redundant
    groups = GROUPS
    hbm = pl.BlockSpec(memory_space=pl.ANY)
    dma = pltpu.SemaphoreType.DMA
    return pl.pallas_call(
        functools.partial(move_kernel, near_count, groups),
        out_shape=jax.ShapeDtypeStruct(
            (buckets, CAPACITY * block + NOTE_ROWS, skeleton), BF16
        ),
        in_specs=[hbm] * 7,
        out_specs=hbm,
        scratch_shapes=[
            pltpu.SMEM((local_count, near_count), jnp.int32),
            pltpu.SMEM((local_count, near_count), jnp.int32),
            pltpu.SMEM((local_count,), jnp.int32),
            pltpu.VMEM((local_count, block, block), BF16),
            pltpu.VMEM((local_count, block, block), BF16),
            pltpu.VMEM((local_count, redundant, redundant), F32),
            pltpu.VMEM((local_count, near_count, block, block), BF16),
            pltpu.VMEM((local_count, skeleton, block), BF16),
            pltpu.VMEM((local_count, near_count, 2 * skeleton, skeleton), BF16),
            pltpu.VMEM((buckets, NOTE_ROWS, skeleton), BF16),
            pltpu.SMEM((buckets,), jnp.int32),
            pltpu.SMEM((local_count, near_count), jnp.int32),
            pltpu.SMEM((buckets, CAPACITY), jnp.int32),
            dma((3,)),
            dma((len(groups), 3)),
            dma((len(groups),)),
            dma((local_count, near_count)),
            dma((1,)),
        ],
        compiler_params=pltpu.CompilerParams(vmem_limit_bytes=56 * 2**20),
        cost_estimate=pl.CostEstimate(
            flops=2 * 10**9, bytes_accessed=13 * 10**6, transcendentals=0
        ),
        name="move_blocks",
    )(col_device, col_local, ranks, bases, diag_blocks, diag_inverses, near_blocks)


def diagonal_kernel(parent, ranks, basis_ref, diag_ref, inverse_ref, out_ref, col_ref):
    c = pl.program_id(0)
    redundant = inverse_ref.shape[1]
    basis = basis_ref[0]
    diagonal = diag_ref[0]
    red = basis[:, :redundant]
    skel = basis[:, redundant:]
    skel_t = skel.T
    left = dot(basis.T, diagonal).astype(BF16)
    upper = dot_wide(inverse_ref[0], dot(left[:redundant], skel))
    lower = dot_wide(dot(left[redundant:], red), inverse_ref[0])
    high, low = halves(upper)
    col = (skel.astype(F32) - (dot(red, high) + dot(red, low))).astype(BF16)
    col_ref[0] = col
    high, low = halves(lower)
    row = (skel_t.astype(F32) - (dot_nt(high, red) + dot_nt(low, red))).astype(BF16)
    reduced = dot(dot(row, diagonal).astype(BF16), col)
    rank = ranks[c]
    rows_at = lax.broadcasted_iota(jnp.int32, reduced.shape, 0)
    cols_at = lax.broadcasted_iota(jnp.int32, reduced.shape, 1)
    keep = (rows_at < rank) & (cols_at < rank)
    out_ref[0] = jnp.where(keep, reduced, 0.0).astype(BF16)


def diagonal_part(bases, diag_blocks, diag_inverses, ranks, parent_group):
    local_count, block, _ = bases.shape
    redundant = diag_inverses.shape[1]
    skeleton = block - redundant

    def own(*shape):
        return pl.BlockSpec((1,) + shape, lambda c, parent, ranks: (c, 0, 0))

    return pl.pallas_call(
        diagonal_kernel,
        out_shape=(
            jax.ShapeDtypeStruct((local_count, skeleton, skeleton), BF16),
            jax.ShapeDtypeStruct((local_count, block, skeleton), BF16),
        ),
        grid_spec=pltpu.PrefetchScalarGridSpec(
            num_scalar_prefetch=2,
            grid=(local_count,),
            in_specs=[
                own(block, block),
                own(block, block),
                own(redundant, redundant),
            ],
            out_specs=[
                pl.BlockSpec(
                    (1, skeleton, skeleton), lambda c, parent, ranks: (parent[c], 0, 0)
                ),
                own(block, skeleton),
            ],
        ),
        compiler_params=pltpu.CompilerParams(vmem_limit_bytes=16 * 2**20),
        cost_estimate=pl.CostEstimate(
            flops=10**9, bytes_accessed=4 * 10**6, transcendentals=0
        ),
        name="diagonal_part",
    )(parent_group[:, 0], ranks, bases, diag_blocks, diag_inverses)


def reduce_kernel(
    chunks,
    ranks_hbm,
    came_hbm,
    col_hbm,
    out_hbm,
    ranks,
    came,
    notes,
    local_rows,
    locals_,
    col,
    out,
    first_sem,
    in_sem,
    out_sem,
):
    skeleton = came.shape[2]
    body = came.shape[1]
    steps = []
    for size in chunks:
        first = steps[-1][-1] + 1 if steps else 0
        steps.append(range(first, first + size))
    ranks_copy = pltpu.make_async_copy(ranks_hbm, ranks, first_sem.at[0])
    col_copy = pltpu.make_async_copy(col_hbm, col, first_sem.at[1])
    note_copy = pltpu.make_async_copy(
        came_hbm.at[:, pl.ds(body, NOTE_ROWS)], notes, first_sem.at[2]
    )
    local_copy = pltpu.make_async_copy(local_rows, locals_, first_sem.at[3])

    def in_copy(i):
        part = pl.ds(steps[i][0], len(steps[i]))
        return pltpu.make_async_copy(
            came_hbm.at[part, pl.ds(0, body)], came.at[part], in_sem.at[i]
        )

    def out_copy(i):
        part = pl.ds(steps[i][0] * CAPACITY, len(steps[i]) * CAPACITY)
        return pltpu.make_async_copy(out.at[part], out_hbm.at[part], out_sem.at[i])

    note_copy.start()
    ranks_copy.start()
    col_copy.start()
    for i in range(len(steps)):
        in_copy(i).start()
    note_copy.wait()
    local_rows[...] = notes[:, 0, :].astype(F32).astype(jnp.int32)
    local_copy.start()
    ranks_copy.wait()
    col_copy.wait()
    local_copy.wait()
    cols_at = lax.broadcasted_iota(jnp.int32, out.shape[1:], 1)

    for i in range(len(steps)):
        in_copy(i).wait()
        for source in steps[i]:
            for s in range(CAPACITY):
                local = locals_[source, s]
                owner = jnp.maximum(local, 0)
                rank = jnp.where(local < 0, 0, ranks[owner])
                top = 2 * s * skeleton
                left = came[source, pl.ds(top, skeleton)]
                right = came[source, pl.ds(top + skeleton, skeleton)]
                product = dot(jnp.concatenate([left, right], 1), col[owner])
                out[source * CAPACITY + s] = jnp.where(cols_at < rank, product, 0.0).astype(BF16)
        out_copy(i).start()
    for i in range(len(steps)):
        out_copy(i).wait()


def reduce_blocks(received, col_basis, ranks):
    sources, rows, skeleton = received.shape
    body = rows - NOTE_ROWS
    chunks = CHUNKS
    hbm = pl.BlockSpec(memory_space=pl.ANY)
    dma = pltpu.SemaphoreType.DMA
    return pl.pallas_call(
        functools.partial(reduce_kernel, chunks),
        out_shape=jax.ShapeDtypeStruct((sources * CAPACITY, skeleton, skeleton), BF16),
        in_specs=[hbm] * 3,
        out_specs=hbm,
        scratch_shapes=[
            pltpu.SMEM(ranks.shape, jnp.int32),
            pltpu.VMEM((sources, body, skeleton), BF16),
            pltpu.VMEM((sources, NOTE_ROWS, skeleton), BF16),
            pltpu.VMEM((sources, skeleton), jnp.int32),
            pltpu.SMEM((sources, skeleton), jnp.int32),
            pltpu.VMEM(col_basis.shape, BF16),
            pltpu.VMEM((sources * CAPACITY, skeleton, skeleton), BF16),
            dma((4,)),
            dma((len(chunks),)),
            dma((len(chunks),)),
        ],
        compiler_params=pltpu.CompilerParams(vmem_limit_bytes=56 * 2**20),
        cost_estimate=pl.CostEstimate(
            flops=6 * 10**8, bytes_accessed=7 * 10**6, transcendentals=0
        ),
        name="reduce_blocks",
    )(ranks, received, col_basis)


def swap_halves(x, axis_name):
    size = lax.axis_size(axis_name)
    me = lax.axis_index(axis_name)
    bit = 1
    while bit < size:
        pairs = x.reshape((size // (2 * bit), 2, bit) + x.shape[1:])
        mine = (me // bit) % 2
        kept = lax.dynamic_index_in_dim(pairs, mine, 1, keepdims=False)
        given = lax.dynamic_index_in_dim(pairs, 1 - mine, 1, keepdims=False)
        got = lax.ppermute(given, axis_name, [(i, i ^ bit) for i in range(size)])
        low, high = jnp.stack([kept, got], 1), jnp.stack([got, kept], 1)
        x = jnp.where(mine == 0, low, high).reshape(x.shape)
        bit *= 2
    return x


def on_device(
    near_blocks, diag_blocks, bases, diag_inverses, col_device, col_local, ranks, parent_group
):
    buckets = lax.axis_size("clu")
    local_count = ranks.shape[0]
    send = move_blocks(
        near_blocks, diag_blocks, bases, diag_inverses, col_device, col_local, ranks, buckets
    )
    skeleton = send.shape[2]
    received = lax.all_to_all(send, "clu", 0, 0, tiled=True)
    outgoing, col_basis = diagonal_part(
        bases, diag_blocks, diag_inverses, ranks, parent_group
    )
    merged = swap_halves(outgoing, "grp").reshape(local_count // 2, 2, skeleton, skeleton)
    reduced = reduce_blocks(received, col_basis, ranks)
    return reduced.reshape(1, buckets, CAPACITY, skeleton, skeleton), merged


def solution(mesh):
    in_specs = (
        P(("grp", "clu"), None, None, None),
        P(("grp", "clu"), None, None),
        P(("grp", "clu"), None, None),
        P(("grp", "clu"), None, None),
        P(("grp", "clu"), None),
        P(("grp", "clu"), None),
        P(("grp", "clu")),
        P(("grp", "clu"), None),
    )
    out_specs = (P(("grp", "clu"), None, None, None, None), P(("grp", "clu"), None, None, None))
    return jax.shard_map(
        on_device, mesh=mesh, in_specs=in_specs, out_specs=out_specs, check_vma=False
    )
```

```python
import functools

import jax
import jax.numpy as jnp
from jax import lax
from jax.experimental import pallas as pl
from jax.experimental.pallas import tpu as pltpu
from jax.sharding import PartitionSpec as P

BF16 = jnp.bfloat16
F32 = jnp.float32
CAPACITY = 2
NEAR_LINKS = 4
HALF_Z = 4


def dot(a, b):
    return jnp.dot(a, b, preferred_element_type=F32)


def dot_nt(a, b):
    return lax.dot_general(a, b, (((1,), (1,)), ((), ())), preferred_element_type=F32)


def halves(x):
    high = x.astype(BF16)
    return high, (x - high.astype(F32)).astype(BF16)


def dot_wide(a, b):
    a_high, a_low = halves(a)
    b_high, b_low = halves(b)
    upper = jnp.concatenate([b_high, b_low], 1)
    lower = jnp.concatenate([b_high, jnp.zeros_like(b_low)], 1)
    both = dot(jnp.concatenate([a_high, a_low], 1), jnp.concatenate([upper, lower], 0))
    return both[:, : b.shape[1]] + both[:, b.shape[1] :]


def move_kernel(
    near_count,
    groups,
    targets_hbm,
    ranks_hbm,
    bases_hbm,
    diag_hbm,
    inverse_hbm,
    near_hbm,
    send_hbm,
    targets,
    ranks,
    bases,
    diag,
    inverse,
    near,
    rows,
    moved,
    count,
    place,
    int_sem,
    in_sem,
    near_sem,
    out_sem,
):
    local_count, block, _ = bases.shape
    redundant = inverse.shape[1]
    skeleton = block - redundant
    members = []
    for size in groups:
        first = members[-1][-1] + 1 if members else 0
        members.append(range(first, first + size))
    ints = (
        pltpu.make_async_copy(targets_hbm, targets, int_sem.at[0]),
        pltpu.make_async_copy(ranks_hbm, ranks, int_sem.at[1]),
    )

    def part(g):
        return pl.ds(members[g][0], len(members[g]))

    def inputs(g):
        return (
            pltpu.make_async_copy(bases_hbm.at[part(g)], bases.at[part(g)], in_sem.at[g, 0]),
            pltpu.make_async_copy(diag_hbm.at[part(g)], diag.at[part(g)], in_sem.at[g, 1]),
            pltpu.make_async_copy(inverse_hbm.at[part(g)], inverse.at[part(g)], in_sem.at[g, 2]),
        )

    def near_copy(g):
        return pltpu.make_async_copy(near_hbm.at[part(g)], near.at[part(g)], near_sem.at[g])

    def out_copy(c, k):
        return pltpu.make_async_copy(moved.at[c, k], send_hbm.at[place[c, k]], out_sem.at[c, k])

    for g in range(len(groups)):
        for copy in inputs(g):
            copy.start()
        if g == 0:
            for copy in ints:
                copy.start()
        near_copy(g).start()

    def clear(d, carry):
        count[d] = 0
        return carry

    lax.fori_loop(0, count.shape[0], clear, 0)
    for copy in ints:
        copy.wait()

    def assign(l, carry):
        for k in range(near_count):
            d = targets[l, k]
            place[l, k] = d * CAPACITY + count[d]
            count[d] = count[d] + 1
        return carry

    lax.fori_loop(0, local_count, assign, 0)

    def prepare(g):
        red = [bases[c][:, :redundant] for c in members[g]]
        skel_t = [bases[c][:, redundant:].T for c in members[g]]
        left = [dot(s, diag[c]).astype(BF16) for s, c in zip(skel_t, members[g])]
        factor = [dot(l, r) for l, r in zip(left, red)]
        lower = [halves(dot_wide(f, inverse[c])) for f, c in zip(factor, members[g])]
        taken = [
            dot_nt(jnp.concatenate(pair, 1), jnp.concatenate([r, r], 1))
            for pair, r in zip(lower, red)
        ]
        for c, s, t in zip(members[g], skel_t, taken):
            rows[c] = (s.astype(F32) - t).astype(BF16)

    rows_at = lax.broadcasted_iota(jnp.int32, (skeleton, block), 0)

    def move(g):
        for c in members[g]:
            keep = rows_at < ranks[c]
            row = rows[c]
            for k in range(near_count):
                moved[c, k] = jnp.where(keep, dot(row, near[c, k]), 0.0).astype(BF16)

    def send_one(c, carry):
        for k in range(near_count):
            out_copy(c, k).start()
        return carry

    def finish_one(c, carry):
        for k in range(near_count):
            out_copy(c, k).wait()
        return carry

    for copy in inputs(0):
        copy.wait()
    prepare(0)
    for g in range(len(groups)):
        near_copy(g).wait()
        if g + 1 < len(groups):
            for copy in inputs(g + 1):
                copy.wait()
        move(g)
        if g + 1 < len(groups):
            prepare(g + 1)
        lax.fori_loop(members[g][0], members[g][-1] + 1, send_one, 0)
    lax.fori_loop(0, local_count, finish_one, 0)


def move_blocks(near_blocks, diag_blocks, bases, diag_inverses, col_device, ranks, buckets):
    local_count, near_count, block, _ = near_blocks.shape
    redundant = diag_inverses.shape[1]
    skeleton = block - redundant
    groups = (2, 4, 2)
    hbm = pl.BlockSpec(memory_space=pl.ANY)
    dma = pltpu.SemaphoreType.DMA
    return pl.pallas_call(
        functools.partial(move_kernel, near_count, groups),
        out_shape=jax.ShapeDtypeStruct((buckets * CAPACITY, skeleton, block), BF16),
        in_specs=[hbm] * 6,
        out_specs=hbm,
        scratch_shapes=[
            pltpu.SMEM((local_count, near_count), jnp.int32),
            pltpu.SMEM((local_count,), jnp.int32),
            pltpu.VMEM((local_count, block, block), BF16),
            pltpu.VMEM((local_count, block, block), BF16),
            pltpu.VMEM((local_count, redundant, redundant), F32),
            pltpu.VMEM((local_count, near_count, block, block), BF16),
            pltpu.VMEM((local_count, skeleton, block), BF16),
            pltpu.VMEM((local_count, near_count, skeleton, block), BF16),
            pltpu.SMEM((buckets,), jnp.int32),
            pltpu.SMEM((local_count, near_count), jnp.int32),
            dma((2,)),
            dma((len(groups), 3)),
            dma((len(groups),)),
            dma((local_count, near_count)),
        ],
        compiler_params=pltpu.CompilerParams(vmem_limit_bytes=56 * 2**20),
        cost_estimate=pl.CostEstimate(
            flops=2 * 10**9, bytes_accessed=13 * 10**6, transcendentals=0
        ),
        name="move_blocks",
    )(col_device, ranks, bases, diag_blocks, diag_inverses, near_blocks)


def table_kernel(me, *refs):
    inputs, table, held, count, sem = refs[:4], refs[4], refs[5:9], refs[9], refs[10]
    copies = [
        pltpu.make_async_copy(ref, place, sem.at[i])
        for i, (ref, place) in enumerate(zip(inputs, held))
    ]
    for copy in copies:
        copy.start()
    device, local, far_device, far_local = held
    local_count, near_count = device.shape
    half = HALF_Z * CAPACITY * 2
    my_side = (me[0] // NEAR_LINKS) % 2

    def blank(x, carry):
        for j in range(2 * half):
            table[x, j] = -1
        return carry

    lax.fori_loop(0, NEAR_LINKS, blank, 0)
    for copy in copies:
        copy.wait()
    for whose, (devices, locals_) in enumerate(((device, local), (far_device, far_local))):

        def clear(d, carry):
            count[d] = 0
            return carry

        def assign(l, carry):
            for k in range(near_count):
                d = devices[l, k]
                z = d // NEAR_LINKS
                away = jnp.where(z % 2 == my_side, 0, half)
                slot = count[d]
                count[d] = slot + 1
                column = (whose * HALF_Z + z // 2) * CAPACITY + slot + away
                table[d % NEAR_LINKS, column] = locals_[l, k]
            return carry

        lax.fori_loop(0, count.shape[0], clear, 0)
        lax.fori_loop(0, local_count, assign, 0)


def make_table(me, device, local, far_device, far_local, buckets):
    smem = pl.BlockSpec(memory_space=pltpu.SMEM)
    hbm = pl.BlockSpec(memory_space=pl.ANY)
    return pl.pallas_call(
        table_kernel,
        out_shape=jax.ShapeDtypeStruct((NEAR_LINKS, HALF_Z * CAPACITY * 4), jnp.int32),
        in_specs=[smem] + [hbm] * 4,
        out_specs=smem,
        scratch_shapes=[pltpu.SMEM(device.shape, jnp.int32)] * 4
        + [pltpu.SMEM((buckets,), jnp.int32), pltpu.SemaphoreType.DMA((4,))],
        compiler_params=pltpu.CompilerParams(vmem_limit_bytes=16 * 2**20),
        name="make_table",
    )(me.reshape(1), device, local, far_device, far_local)


def diagonal_kernel(parent, ranks, basis_ref, diag_ref, inverse_ref, out_ref, col_ref):
    c = pl.program_id(0)
    redundant = inverse_ref.shape[1]
    basis = basis_ref[0]
    diagonal = diag_ref[0]
    red = basis[:, :redundant]
    skel = basis[:, redundant:]
    skel_t = skel.T
    left = dot(basis.T, diagonal).astype(BF16)
    upper = dot_wide(inverse_ref[0], dot(left[:redundant], skel))
    lower = dot_wide(dot(left[redundant:], red), inverse_ref[0])
    high, low = halves(upper)
    col = (skel.astype(F32) - (dot(red, high) + dot(red, low))).astype(BF16)
    col_ref[0] = col
    high, low = halves(lower)
    row = (skel_t.astype(F32) - (dot_nt(high, red) + dot_nt(low, red))).astype(BF16)
    reduced = dot(dot(row, diagonal).astype(BF16), col)
    rank = ranks[c]
    rows_at = lax.broadcasted_iota(jnp.int32, reduced.shape, 0)
    cols_at = lax.broadcasted_iota(jnp.int32, reduced.shape, 1)
    keep = (rows_at < rank) & (cols_at < rank)
    out_ref[0] = jnp.where(keep, reduced, 0.0).astype(BF16)


def diagonal_part(bases, diag_blocks, diag_inverses, ranks, parent_group):
    local_count, block, _ = bases.shape
    redundant = diag_inverses.shape[1]
    skeleton = block - redundant

    def own(*shape):
        return pl.BlockSpec((1,) + shape, lambda c, parent, ranks: (c, 0, 0))

    return pl.pallas_call(
        diagonal_kernel,
        out_shape=(
            jax.ShapeDtypeStruct((local_count, skeleton, skeleton), BF16),
            jax.ShapeDtypeStruct((local_count, block, skeleton), BF16),
        ),
        grid_spec=pltpu.PrefetchScalarGridSpec(
            num_scalar_prefetch=2,
            grid=(local_count,),
            in_specs=[
                own(block, block),
                own(block, block),
                own(redundant, redundant),
            ],
            out_specs=[
                pl.BlockSpec(
                    (1, skeleton, skeleton), lambda c, parent, ranks: (parent[c], 0, 0)
                ),
                own(block, skeleton),
            ],
        ),
        compiler_params=pltpu.CompilerParams(vmem_limit_bytes=16 * 2**20),
        cost_estimate=pl.CostEstimate(
            flops=10**9, bytes_accessed=4 * 10**6, transcendentals=0
        ),
        name="diagonal_part",
    )(parent_group[:, 0], ranks, bases, diag_blocks, diag_inverses)


def reduce_kernel(chunk, far, *refs):
    tables_hbm = refs[:far]
    (
        me_hbm,
        ranks_hbm,
        moved_hbm,
        col_hbm,
        out_hbm,
        tables,
        me,
        ranks,
        moved,
        col,
        out,
        table_sem,
        int_sem,
        in_sem,
        out_sem,
    ) = refs[far:]
    steps = moved.shape[0] // chunk
    firsts = (
        pltpu.make_async_copy(me_hbm, me, int_sem.at[0]),
        pltpu.make_async_copy(ranks_hbm, ranks, int_sem.at[1]),
        pltpu.make_async_copy(col_hbm, col, int_sem.at[2]),
    ) + tuple(
        pltpu.make_async_copy(tables_hbm[t], tables.at[t], table_sem.at[t]) for t in range(far)
    )

    def in_copy(i):
        part = pl.ds(i * chunk, chunk)
        return pltpu.make_async_copy(moved_hbm.at[part], moved.at[part], in_sem.at[i])

    def out_copy(i):
        part = pl.ds(i * chunk, chunk)
        return pltpu.make_async_copy(out.at[part], out_hbm.at[part], out_sem.at[i])

    for copy in firsts:
        copy.start()
    for i in range(steps):
        in_copy(i).start()
    for copy in firsts:
        copy.wait()
    cols_at = lax.broadcasted_iota(jnp.int32, out.shape[1:], 1)
    my_z = me[0] // NEAR_LINKS

    for i in range(steps):
        in_copy(i).wait()
        for e in range(i * chunk, (i + 1) * chunk):
            source = e // CAPACITY
            apart = (source // NEAR_LINKS) ^ my_z
            column = (apart % 2) * CAPACITY + e % CAPACITY
            local = tables[apart // 2, source % NEAR_LINKS, column]
            owner = jnp.maximum(local, 0)
            rank = jnp.where(local < 0, 0, ranks[owner])
            out[e] = jnp.where(cols_at < rank, dot(moved[e], col[owner]), 0.0).astype(BF16)
        out_copy(i).start()
    for i in range(steps):
        out_copy(i).wait()


def reduce_blocks(moved, tables, me, col_basis, ranks):
    slots, skeleton, block = moved.shape
    far = len(tables)
    chunk = 32
    hbm = pl.BlockSpec(memory_space=pl.ANY)
    dma = pltpu.SemaphoreType.DMA
    return pl.pallas_call(
        functools.partial(reduce_kernel, chunk, far),
        out_shape=jax.ShapeDtypeStruct((slots, skeleton, skeleton), BF16),
        in_specs=[hbm] * (far + 4),
        out_specs=hbm,
        scratch_shapes=[
            pltpu.SMEM((far,) + tables[0].shape, jnp.int32),
            pltpu.SMEM((1,), jnp.int32),
            pltpu.SMEM(ranks.shape, jnp.int32),
            pltpu.VMEM(moved.shape, BF16),
            pltpu.VMEM(col_basis.shape, BF16),
            pltpu.VMEM((slots, skeleton, skeleton), BF16),
            dma((far,)),
            dma((3,)),
            dma((slots // chunk,)),
            dma((slots // chunk,)),
        ],
        compiler_params=pltpu.CompilerParams(vmem_limit_bytes=12 * 2**20),
        cost_estimate=pl.CostEstimate(
            flops=6 * 10**8, bytes_accessed=7 * 10**6, transcendentals=0
        ),
        name="reduce_blocks",
    )(*tables, me.reshape(1), ranks, moved, col_basis)


def swap_halves(x, axis_name, size):
    whole = lax.axis_size(axis_name)
    me = lax.axis_index(axis_name)
    bit = 1
    while bit < size:
        pairs = x.reshape((size // (2 * bit), 2, bit) + x.shape[1:])
        mine = (me // bit) % 2
        kept = lax.dynamic_index_in_dim(pairs, mine, 1, keepdims=False)
        given = lax.dynamic_index_in_dim(pairs, 1 - mine, 1, keepdims=False)
        got = lax.ppermute(given, axis_name, [(i, i ^ bit) for i in range(whole)])
        low, high = jnp.stack([kept, got], 1), jnp.stack([got, kept], 1)
        x = jnp.where(mine == 0, low, high).reshape(x.shape)
        bit *= 2
    return x


def on_device(
    near_blocks, diag_blocks, bases, diag_inverses, col_device, col_local, ranks, parent_group
):
    buckets = lax.axis_size("clu")
    local_count = ranks.shape[0]
    me = lax.axis_index("clu")
    across = [(i, i ^ NEAR_LINKS) for i in range(buckets)]
    far_device = lax.ppermute(col_device, "clu", across)
    far_local = lax.ppermute(col_local, "clu", across)
    send = move_blocks(
        near_blocks, diag_blocks, bases, diag_inverses, col_device, ranks, buckets
    )
    send, far_device, far_local = lax.optimization_barrier((send, far_device, far_local))
    skeleton, block = send.shape[1:]
    received = lax.all_to_all(
        send.reshape(buckets, CAPACITY, skeleton, block), "clu", 0, 0, tiled=True
    )
    outgoing, col_basis = diagonal_part(
        bases, diag_blocks, diag_inverses, ranks, parent_group
    )
    arrived = swap_halves(outgoing, "grp", lax.axis_size("grp"))
    merged = arrived.reshape(local_count // 2, 2, skeleton, skeleton)

    table = make_table(me, col_device, col_local, far_device, far_local, buckets)
    table = swap_halves(table, "clu", NEAR_LINKS)
    table, merged = lax.optimization_barrier((table, merged))
    table = table[:, : 2 * HALF_Z * CAPACITY].reshape(NEAR_LINKS, 2, HALF_Z, CAPACITY)
    my_place = me // (2 * NEAR_LINKS)
    tables = []
    for apart in range(HALF_Z):
        given = lax.dynamic_index_in_dim(table, my_place ^ apart, 2, keepdims=False)
        given = given.reshape(NEAR_LINKS, 2 * CAPACITY)
        if apart:
            pairs = [(i, i ^ (2 * apart * NEAR_LINKS)) for i in range(buckets)]
            given = lax.ppermute(given, "clu", pairs)
        tables.append(given)
    reduced = reduce_blocks(
        received.reshape(buckets * CAPACITY, skeleton, block), tables, me, col_basis, ranks
    )
    return reduced.reshape(1, buckets, CAPACITY, skeleton, skeleton), merged


def solution(mesh):
    in_specs = (
        P(("grp", "clu"), None, None, None),
        P(("grp", "clu"), None, None),
        P(("grp", "clu"), None, None),
        P(("grp", "clu"), None, None),
        P(("grp", "clu"), None),
        P(("grp", "clu"), None),
        P(("grp", "clu")),
        P(("grp", "clu"), None),
    )
    out_specs = (P(("grp", "clu"), None, None, None, None), P(("grp", "clu"), None, None, None))
    return jax.shard_map(
        on_device, mesh=mesh, in_specs=in_specs, out_specs=out_specs, check_vma=False
    )
```

```python
import functools

import jax
import jax.numpy as jnp
from jax import lax
from jax.experimental import pallas as pl
from jax.experimental.pallas import tpu as pltpu
from jax.sharding import PartitionSpec as P

BF16 = jnp.bfloat16
F32 = jnp.float32
CAPACITY = 2
PIECE = 8
NEAR_LINKS = 4
HALF_Z = 4


def dot(a, b):
    return jnp.dot(a, b, preferred_element_type=F32)


def dot_nt(a, b):
    return lax.dot_general(a, b, (((1,), (1,)), ((), ())), preferred_element_type=F32)


def halves(x):
    high = x.astype(BF16)
    return high, (x - high.astype(F32)).astype(BF16)


def dot_wide(a, b):
    a_high, a_low = halves(a)
    b_high, b_low = halves(b)
    upper = jnp.concatenate([b_high, b_low], 1)
    lower = jnp.concatenate([b_high, jnp.zeros_like(b_low)], 1)
    both = dot(jnp.concatenate([a_high, a_low], 1), jnp.concatenate([upper, lower], 0))
    return both[:, : b.shape[1]] + both[:, b.shape[1] :]


def move_kernel(
    near_count,
    groups,
    targets_hbm,
    ranks_hbm,
    bases_hbm,
    diag_hbm,
    inverse_hbm,
    near_hbm,
    send_hbm,
    targets,
    ranks,
    bases,
    diag,
    inverse,
    near,
    rows,
    moved,
    count,
    place,
    int_sem,
    in_sem,
    near_sem,
    out_sem,
):
    local_count, block, _ = bases.shape
    redundant = inverse.shape[1]
    skeleton = block - redundant
    members = []
    for size in groups:
        first = members[-1][-1] + 1 if members else 0
        members.append(range(first, first + size))
    ints = (
        pltpu.make_async_copy(targets_hbm, targets, int_sem.at[0]),
        pltpu.make_async_copy(ranks_hbm, ranks, int_sem.at[1]),
    )

    def part(g):
        return pl.ds(members[g][0], len(members[g]))

    def inputs(g):
        return (
            pltpu.make_async_copy(bases_hbm.at[part(g)], bases.at[part(g)], in_sem.at[g, 0]),
            pltpu.make_async_copy(diag_hbm.at[part(g)], diag.at[part(g)], in_sem.at[g, 1]),
            pltpu.make_async_copy(inverse_hbm.at[part(g)], inverse.at[part(g)], in_sem.at[g, 2]),
        )

    def near_copy(g):
        return pltpu.make_async_copy(near_hbm.at[part(g)], near.at[part(g)], near_sem.at[g])

    def out_copy(c, k):
        return pltpu.make_async_copy(moved.at[c, k], send_hbm.at[place[c, k]], out_sem.at[c, k])

    for g in range(len(groups)):
        for copy in inputs(g):
            copy.start()
        if g == 0:
            for copy in ints:
                copy.start()
        near_copy(g).start()

    def clear(d, carry):
        count[d] = 0
        return carry

    lax.fori_loop(0, count.shape[0], clear, 0)
    for copy in ints:
        copy.wait()

    def assign(l, carry):
        for k in range(near_count):
            d = targets[l, k]
            place[l, k] = d * CAPACITY + count[d]
            count[d] = count[d] + 1
        return carry

    lax.fori_loop(0, local_count, assign, 0)

    def prepare(g):
        red = [bases[c][:, :redundant] for c in members[g]]
        skel_t = [bases[c][:, redundant:].T for c in members[g]]
        left = [dot(s, diag[c]).astype(BF16) for s, c in zip(skel_t, members[g])]
        factor = [dot(l, r) for l, r in zip(left, red)]
        lower = [halves(dot_wide(f, inverse[c])) for f, c in zip(factor, members[g])]
        taken = [
            dot_nt(jnp.concatenate(pair, 1), jnp.concatenate([r, r], 1))
            for pair, r in zip(lower, red)
        ]
        for c, s, t in zip(members[g], skel_t, taken):
            rows[c] = (s.astype(F32) - t).astype(BF16)

    rows_at = lax.broadcasted_iota(jnp.int32, (skeleton, block), 0)

    def move(g):
        for c in members[g]:
            keep = rows_at < ranks[c]
            row = rows[c]
            for k in range(near_count):
                moved[c, k] = jnp.where(keep, dot(row, near[c, k]), 0.0).astype(BF16)
            for k in range(near_count):
                out_copy(c, k).start()

    def finish_one(c, carry):
        for k in range(near_count):
            out_copy(c, k).wait()
        return carry

    for copy in inputs(0):
        copy.wait()
    prepare(0)
    for g in range(len(groups)):
        near_copy(g).wait()
        if g + 1 < len(groups):
            for copy in inputs(g + 1):
                copy.wait()
        move(g)
        if g + 1 < len(groups):
            prepare(g + 1)
    lax.fori_loop(0, local_count, finish_one, 0)


def move_blocks(near_blocks, diag_blocks, bases, diag_inverses, col_device, ranks, buckets):
    local_count, near_count, block, _ = near_blocks.shape
    redundant = diag_inverses.shape[1]
    skeleton = block - redundant
    groups = (4, 4)
    hbm = pl.BlockSpec(memory_space=pl.ANY)
    dma = pltpu.SemaphoreType.DMA
    return pl.pallas_call(
        functools.partial(move_kernel, near_count, groups),
        out_shape=jax.ShapeDtypeStruct((buckets * CAPACITY, skeleton, block), BF16),
        in_specs=[hbm] * 6,
        out_specs=hbm,
        scratch_shapes=[
            pltpu.SMEM((local_count, near_count), jnp.int32),
            pltpu.SMEM((local_count,), jnp.int32),
            pltpu.VMEM((local_count, block, block), BF16),
            pltpu.VMEM((local_count, block, block), BF16),
            pltpu.VMEM((local_count, redundant, redundant), F32),
            pltpu.VMEM((local_count, near_count, block, block), BF16),
            pltpu.VMEM((local_count, skeleton, block), BF16),
            pltpu.VMEM((local_count, near_count, skeleton, block), BF16),
            pltpu.SMEM((buckets,), jnp.int32),
            pltpu.SMEM((local_count, near_count), jnp.int32),
            dma((2,)),
            dma((len(groups), 3)),
            dma((len(groups),)),
            dma((local_count, near_count)),
        ],
        compiler_params=pltpu.CompilerParams(vmem_limit_bytes=56 * 2**20),
        cost_estimate=pl.CostEstimate(
            flops=2 * 10**9, bytes_accessed=13 * 10**6, transcendentals=0
        ),
        name="move_blocks",
    )(col_device, ranks, bases, diag_blocks, diag_inverses, near_blocks)


def table_kernel(me, *refs):
    inputs, table, held, count, sem = refs[:4], refs[4], refs[5:9], refs[9], refs[10]
    copies = [
        pltpu.make_async_copy(ref, place, sem.at[i])
        for i, (ref, place) in enumerate(zip(inputs, held))
    ]
    for copy in copies:
        copy.start()
    device, local, far_device, far_local = held
    local_count, near_count = device.shape
    half = HALF_Z * CAPACITY * 2
    my_side = (me[0] // NEAR_LINKS) % 2

    def blank(x, carry):
        for j in range(2 * half):
            table[x, j] = -1
        return carry

    lax.fori_loop(0, NEAR_LINKS, blank, 0)
    for copy in copies:
        copy.wait()
    for whose, (devices, locals_) in enumerate(((device, local), (far_device, far_local))):

        def clear(d, carry):
            count[d] = 0
            return carry

        def assign(l, carry):
            for k in range(near_count):
                d = devices[l, k]
                z = d // NEAR_LINKS
                away = jnp.where(z % 2 == my_side, 0, half)
                slot = count[d]
                count[d] = slot + 1
                column = (whose * HALF_Z + z // 2) * CAPACITY + slot + away
                table[d % NEAR_LINKS, column] = locals_[l, k]
            return carry

        lax.fori_loop(0, count.shape[0], clear, 0)
        lax.fori_loop(0, local_count, assign, 0)


def make_table(me, device, local, far_device, far_local, buckets):
    smem = pl.BlockSpec(memory_space=pltpu.SMEM)
    hbm = pl.BlockSpec(memory_space=pl.ANY)
    return pl.pallas_call(
        table_kernel,
        out_shape=jax.ShapeDtypeStruct((NEAR_LINKS, HALF_Z * CAPACITY * 4), jnp.int32),
        in_specs=[smem] + [hbm] * 4,
        out_specs=smem,
        scratch_shapes=[pltpu.SMEM(device.shape, jnp.int32)] * 4
        + [pltpu.SMEM((buckets,), jnp.int32), pltpu.SemaphoreType.DMA((4,))],
        compiler_params=pltpu.CompilerParams(vmem_limit_bytes=16 * 2**20),
        name="make_table",
    )(me.reshape(1), device, local, far_device, far_local)


def diagonal_kernel(parent, ranks, basis_ref, diag_ref, inverse_ref, out_ref, col_ref):
    c = pl.program_id(0)
    redundant = inverse_ref.shape[1]
    basis = basis_ref[0]
    diagonal = diag_ref[0]
    red = basis[:, :redundant]
    skel = basis[:, redundant:]
    skel_t = skel.T
    left = dot(basis.T, diagonal).astype(BF16)
    upper = dot_wide(inverse_ref[0], dot(left[:redundant], skel))
    lower = dot_wide(dot(left[redundant:], red), inverse_ref[0])
    high, low = halves(upper)
    col = (skel.astype(F32) - (dot(red, high) + dot(red, low))).astype(BF16)
    col_ref[0] = col
    high, low = halves(lower)
    row = (skel_t.astype(F32) - (dot_nt(high, red) + dot_nt(low, red))).astype(BF16)
    reduced = dot(dot(row, diagonal).astype(BF16), col)
    rank = ranks[c]
    rows_at = lax.broadcasted_iota(jnp.int32, reduced.shape, 0)
    cols_at = lax.broadcasted_iota(jnp.int32, reduced.shape, 1)
    keep = (rows_at < rank) & (cols_at < rank)
    out_ref[0] = jnp.where(keep, reduced, 0.0).astype(BF16)


def diagonal_part(bases, diag_blocks, diag_inverses, ranks, parent_group):
    local_count, block, _ = bases.shape
    redundant = diag_inverses.shape[1]
    skeleton = block - redundant

    def own(*shape):
        return pl.BlockSpec((1,) + shape, lambda c, parent, ranks: (c, 0, 0))

    return pl.pallas_call(
        diagonal_kernel,
        out_shape=(
            jax.ShapeDtypeStruct((local_count, skeleton, skeleton), BF16),
            jax.ShapeDtypeStruct((local_count, block, skeleton), BF16),
        ),
        grid_spec=pltpu.PrefetchScalarGridSpec(
            num_scalar_prefetch=2,
            grid=(local_count,),
            in_specs=[
                own(block, block),
                own(block, block),
                own(redundant, redundant),
            ],
            out_specs=[
                pl.BlockSpec(
                    (1, skeleton, skeleton), lambda c, parent, ranks: (parent[c], 0, 0)
                ),
                own(block, skeleton),
            ],
        ),
        compiler_params=pltpu.CompilerParams(vmem_limit_bytes=16 * 2**20),
        cost_estimate=pl.CostEstimate(
            flops=10**9, bytes_accessed=4 * 10**6, transcendentals=0
        ),
        name="diagonal_part",
    )(parent_group[:, 0], ranks, bases, diag_blocks, diag_inverses)


def reduce_kernel(chunk, far, *refs):
    tables_hbm = refs[:far]
    (
        me_hbm,
        ranks_hbm,
        moved_hbm,
        col_hbm,
        out_hbm,
        tables,
        me,
        ranks,
        moved,
        col,
        out,
        table_sem,
        int_sem,
        in_sem,
        out_sem,
    ) = refs[far:]
    steps = moved.shape[0] // chunk
    firsts = (
        pltpu.make_async_copy(me_hbm, me, int_sem.at[0]),
        pltpu.make_async_copy(ranks_hbm, ranks, int_sem.at[1]),
        pltpu.make_async_copy(col_hbm, col, int_sem.at[2]),
    ) + tuple(
        pltpu.make_async_copy(tables_hbm[t], tables.at[t], table_sem.at[t]) for t in range(far)
    )

    def in_copy(i):
        part = pl.ds(i * chunk, chunk)
        return pltpu.make_async_copy(moved_hbm.at[part], moved.at[part], in_sem.at[i])

    def out_copy(i):
        part = pl.ds(i * PIECE, PIECE)
        return pltpu.make_async_copy(out.at[part], out_hbm.at[part], out_sem.at[i])

    for copy in firsts:
        copy.start()
    for i in range(steps):
        in_copy(i).start()
    for copy in firsts:
        copy.wait()
    cols_at = lax.broadcasted_iota(jnp.int32, out.shape[1:], 1)
    my_z = me[0] // NEAR_LINKS

    for i in range(steps):
        in_copy(i).wait()
        for e in range(i * chunk, (i + 1) * chunk):
            source = e // CAPACITY
            apart = (source // NEAR_LINKS) ^ my_z
            column = (apart % 2) * CAPACITY + e % CAPACITY
            local = tables[apart // 2, source % NEAR_LINKS, column]
            owner = jnp.maximum(local, 0)
            rank = jnp.where(local < 0, 0, ranks[owner])
            out[e] = jnp.where(cols_at < rank, dot(moved[e], col[owner]), 0.0).astype(BF16)
            if e % PIECE == PIECE - 1:
                out_copy(e // PIECE).start()
    for i in range(moved.shape[0] // PIECE):
        out_copy(i).wait()


def reduce_blocks(moved, tables, me, col_basis, ranks):
    slots, skeleton, block = moved.shape
    far = len(tables)
    chunk = 32
    hbm = pl.BlockSpec(memory_space=pl.ANY)
    dma = pltpu.SemaphoreType.DMA
    return pl.pallas_call(
        functools.partial(reduce_kernel, chunk, far),
        out_shape=jax.ShapeDtypeStruct((slots, skeleton, skeleton), BF16),
        in_specs=[hbm] * (far + 4),
        out_specs=hbm,
        scratch_shapes=[
            pltpu.SMEM((far,) + tables[0].shape, jnp.int32),
            pltpu.SMEM((1,), jnp.int32),
            pltpu.SMEM(ranks.shape, jnp.int32),
            pltpu.VMEM(moved.shape, BF16),
            pltpu.VMEM(col_basis.shape, BF16),
            pltpu.VMEM((slots, skeleton, skeleton), BF16),
            dma((far,)),
            dma((3,)),
            dma((slots // chunk,)),
            dma((slots // PIECE,)),
        ],
        compiler_params=pltpu.CompilerParams(vmem_limit_bytes=12 * 2**20),
        cost_estimate=pl.CostEstimate(
            flops=6 * 10**8, bytes_accessed=7 * 10**6, transcendentals=0
        ),
        name="reduce_blocks",
    )(*tables, me.reshape(1), ranks, moved, col_basis)


def swap_halves(x, axis_name, size):
    whole = lax.axis_size(axis_name)
    me = lax.axis_index(axis_name)
    bit = 1
    while bit < size:
        pairs = x.reshape((size // (2 * bit), 2, bit) + x.shape[1:])
        mine = (me // bit) % 2
        kept = lax.dynamic_index_in_dim(pairs, mine, 1, keepdims=False)
        given = lax.dynamic_index_in_dim(pairs, 1 - mine, 1, keepdims=False)
        got = lax.ppermute(given, axis_name, [(i, i ^ bit) for i in range(whole)])
        low, high = jnp.stack([kept, got], 1), jnp.stack([got, kept], 1)
        x = jnp.where(mine == 0, low, high).reshape(x.shape)
        bit *= 2
    return x


def on_device(
    near_blocks, diag_blocks, bases, diag_inverses, col_device, col_local, ranks, parent_group
):
    buckets = lax.axis_size("clu")
    local_count = ranks.shape[0]
    me = lax.axis_index("clu")
    across = [(i, i ^ NEAR_LINKS) for i in range(buckets)]
    far_device = lax.ppermute(col_device, "clu", across)
    far_local = lax.ppermute(col_local, "clu", across)
    send = move_blocks(
        near_blocks, diag_blocks, bases, diag_inverses, col_device, ranks, buckets
    )
    send, far_device, far_local = lax.optimization_barrier((send, far_device, far_local))
    skeleton, block = send.shape[1:]
    received = lax.all_to_all(
        send.reshape(buckets, CAPACITY, skeleton, block), "clu", 0, 0, tiled=True
    )
    outgoing, col_basis = diagonal_part(
        bases, diag_blocks, diag_inverses, ranks, parent_group
    )
    arrived = swap_halves(outgoing, "grp", lax.axis_size("grp"))
    merged = arrived.reshape(local_count // 2, 2, skeleton, skeleton)

    table = make_table(me, col_device, col_local, far_device, far_local, buckets)
    table = swap_halves(table, "clu", NEAR_LINKS)
    table, merged = lax.optimization_barrier((table, merged))
    table = table[:, : 2 * HALF_Z * CAPACITY].reshape(NEAR_LINKS, 2, HALF_Z, CAPACITY)
    my_place = me // (2 * NEAR_LINKS)
    tables = []
    for apart in range(HALF_Z):
        given = lax.dynamic_index_in_dim(table, my_place ^ apart, 2, keepdims=False)
        given = given.reshape(NEAR_LINKS, 2 * CAPACITY)
        if apart:
            pairs = [(i, i ^ (2 * apart * NEAR_LINKS)) for i in range(buckets)]
            given = lax.ppermute(given, "clu", pairs)
        tables.append(given)
    reduced = reduce_blocks(
        received.reshape(buckets * CAPACITY, skeleton, block), tables, me, col_basis, ranks
    )
    return reduced.reshape(1, buckets, CAPACITY, skeleton, skeleton), merged


def solution(mesh):
    in_specs = (
        P(("grp", "clu"), None, None, None),
        P(("grp", "clu"), None, None),
        P(("grp", "clu"), None, None),
        P(("grp", "clu"), None, None),
        P(("grp", "clu"), None),
        P(("grp", "clu"), None),
        P(("grp", "clu")),
        P(("grp", "clu"), None),
    )
    out_specs = (P(("grp", "clu"), None, None, None, None), P(("grp", "clu"), None, None, None))
    return jax.shard_map(
        on_device, mesh=mesh, in_specs=in_specs, out_specs=out_specs, check_vma=False
    )
```

```python
import functools

import jax
import jax.numpy as jnp
from jax import lax
from jax.experimental import pallas as pl
from jax.experimental.pallas import tpu as pltpu
from jax.sharding import PartitionSpec as P

BF16 = jnp.bfloat16
F32 = jnp.float32
CAPACITY = 2
PIECE = 8
NEAR_LINKS = 4
HALF_Z = 4


def dot(a, b):
    return jnp.dot(a, b, preferred_element_type=F32)


def dot_nt(a, b):
    return lax.dot_general(a, b, (((1,), (1,)), ((), ())), preferred_element_type=F32)


def halves(x):
    high = x.astype(BF16)
    return high, (x - high.astype(F32)).astype(BF16)


def dot_wide(a, b):
    a_high, a_low = halves(a)
    b_high, b_low = halves(b)
    upper = jnp.concatenate([b_high, b_low], 1)
    lower = jnp.concatenate([b_high, jnp.zeros_like(b_low)], 1)
    both = dot(jnp.concatenate([a_high, a_low], 1), jnp.concatenate([upper, lower], 0))
    return both[:, : b.shape[1]] + both[:, b.shape[1] :]


def move_kernel(
    near_count,
    groups,
    targets_hbm,
    ranks_hbm,
    bases_hbm,
    diag_hbm,
    inverse_hbm,
    near_hbm,
    send_hbm,
    targets,
    ranks,
    bases,
    diag,
    inverse,
    near,
    rows,
    moved,
    count,
    place,
    int_sem,
    in_sem,
    near_sem,
    out_sem,
):
    local_count, block, _ = bases.shape
    redundant = inverse.shape[1]
    skeleton = block - redundant
    members = []
    for size in groups:
        first = members[-1][-1] + 1 if members else 0
        members.append(range(first, first + size))
    ints = (
        pltpu.make_async_copy(targets_hbm, targets, int_sem.at[0]),
        pltpu.make_async_copy(ranks_hbm, ranks, int_sem.at[1]),
    )

    def part(g):
        return pl.ds(members[g][0], len(members[g]))

    def inputs(g):
        return (
            pltpu.make_async_copy(bases_hbm.at[part(g)], bases.at[part(g)], in_sem.at[g, 0]),
            pltpu.make_async_copy(diag_hbm.at[part(g)], diag.at[part(g)], in_sem.at[g, 1]),
            pltpu.make_async_copy(inverse_hbm.at[part(g)], inverse.at[part(g)], in_sem.at[g, 2]),
        )

    def near_copy(g):
        return pltpu.make_async_copy(near_hbm.at[part(g)], near.at[part(g)], near_sem.at[g])

    def out_copy(c, k):
        return pltpu.make_async_copy(moved.at[c, k], send_hbm.at[place[c, k]], out_sem.at[c, k])

    for g in range(len(groups)):
        for copy in inputs(g):
            copy.start()
        if g == 0:
            for copy in ints:
                copy.start()
        near_copy(g).start()

    def clear(d, carry):
        count[d] = 0
        return carry

    lax.fori_loop(0, count.shape[0], clear, 0)
    for copy in ints:
        copy.wait()

    def assign(l, carry):
        for k in range(near_count):
            d = targets[l, k]
            place[l, k] = d * CAPACITY + count[d]
            count[d] = count[d] + 1
        return carry

    lax.fori_loop(0, local_count, assign, 0)

    def prepare(g):
        red = [bases[c][:, :redundant] for c in members[g]]
        skel_t = [bases[c][:, redundant:].T for c in members[g]]
        left = [dot(s, diag[c]).astype(BF16) for s, c in zip(skel_t, members[g])]
        factor = [dot(l, r) for l, r in zip(left, red)]
        lower = [halves(dot_wide(f, inverse[c])) for f, c in zip(factor, members[g])]
        taken = [
            dot_nt(jnp.concatenate(pair, 1), jnp.concatenate([r, r], 1))
            for pair, r in zip(lower, red)
        ]
        for c, s, t in zip(members[g], skel_t, taken):
            rows[c] = (s.astype(F32) - t).astype(BF16)

    rows_at = lax.broadcasted_iota(jnp.int32, (skeleton, block), 0)

    def move(g):
        for c in members[g]:
            keep = rows_at < ranks[c]
            row = rows[c]
            for k in range(near_count):
                moved[c, k] = jnp.where(keep, dot(row, near[c, k]), 0.0).astype(BF16)
            for k in range(near_count):
                out_copy(c, k).start()

    def finish_one(c, carry):
        for k in range(near_count):
            out_copy(c, k).wait()
        return carry

    for copy in inputs(0):
        copy.wait()
    prepare(0)
    for g in range(len(groups)):
        near_copy(g).wait()
        if g + 1 < len(groups):
            for copy in inputs(g + 1):
                copy.wait()
        move(g)
        if g + 1 < len(groups):
            prepare(g + 1)
    lax.fori_loop(0, local_count, finish_one, 0)


def move_blocks(near_blocks, diag_blocks, bases, diag_inverses, col_device, ranks, buckets):
    local_count, near_count, block, _ = near_blocks.shape
    redundant = diag_inverses.shape[1]
    skeleton = block - redundant
    groups = (4, 4)
    hbm = pl.BlockSpec(memory_space=pl.ANY)
    dma = pltpu.SemaphoreType.DMA
    return pl.pallas_call(
        functools.partial(move_kernel, near_count, groups),
        out_shape=jax.ShapeDtypeStruct((buckets * CAPACITY, skeleton, block), BF16),
        in_specs=[hbm] * 6,
        out_specs=hbm,
        scratch_shapes=[
            pltpu.SMEM((local_count, near_count), jnp.int32),
            pltpu.SMEM((local_count,), jnp.int32),
            pltpu.VMEM((local_count, block, block), BF16),
            pltpu.VMEM((local_count, block, block), BF16),
            pltpu.VMEM((local_count, redundant, redundant), F32),
            pltpu.VMEM((local_count, near_count, block, block), BF16),
            pltpu.VMEM((local_count, skeleton, block), BF16),
            pltpu.VMEM((local_count, near_count, skeleton, block), BF16),
            pltpu.SMEM((buckets,), jnp.int32),
            pltpu.SMEM((local_count, near_count), jnp.int32),
            dma((2,)),
            dma((len(groups), 3)),
            dma((len(groups),)),
            dma((local_count, near_count)),
        ],
        compiler_params=pltpu.CompilerParams(vmem_limit_bytes=56 * 2**20),
        cost_estimate=pl.CostEstimate(
            flops=2 * 10**9, bytes_accessed=13 * 10**6, transcendentals=0
        ),
        name="move_blocks",
    )(col_device, ranks, bases, diag_blocks, diag_inverses, near_blocks)


def table_kernel(me, *refs):
    inputs, table, held, count, sem = refs[:4], refs[4], refs[5:9], refs[9], refs[10]
    copies = [
        pltpu.make_async_copy(ref, place, sem.at[i])
        for i, (ref, place) in enumerate(zip(inputs, held))
    ]
    for copy in copies:
        copy.start()
    device, local, far_device, far_local = held
    local_count, near_count = device.shape
    half = HALF_Z * CAPACITY * 2
    my_side = (me[0] // NEAR_LINKS) % 2

    def blank(x, carry):
        for j in range(2 * half):
            table[x, j] = -1
        return carry

    lax.fori_loop(0, NEAR_LINKS, blank, 0)
    for copy in copies:
        copy.wait()
    for whose, (devices, locals_) in enumerate(((device, local), (far_device, far_local))):

        def clear(d, carry):
            count[d] = 0
            return carry

        def assign(l, carry):
            for k in range(near_count):
                d = devices[l, k]
                z = d // NEAR_LINKS
                away = jnp.where(z % 2 == my_side, 0, half)
                slot = count[d]
                count[d] = slot + 1
                column = (whose * HALF_Z + z // 2) * CAPACITY + slot + away
                table[d % NEAR_LINKS, column] = locals_[l, k]
            return carry

        lax.fori_loop(0, count.shape[0], clear, 0)
        lax.fori_loop(0, local_count, assign, 0)


def make_table(me, device, local, far_device, far_local, buckets):
    smem = pl.BlockSpec(memory_space=pltpu.SMEM)
    hbm = pl.BlockSpec(memory_space=pl.ANY)
    return pl.pallas_call(
        table_kernel,
        out_shape=jax.ShapeDtypeStruct((NEAR_LINKS, HALF_Z * CAPACITY * 4), jnp.int32),
        in_specs=[smem] + [hbm] * 4,
        out_specs=smem,
        scratch_shapes=[pltpu.SMEM(device.shape, jnp.int32)] * 4
        + [pltpu.SMEM((buckets,), jnp.int32), pltpu.SemaphoreType.DMA((4,))],
        compiler_params=pltpu.CompilerParams(vmem_limit_bytes=16 * 2**20),
        name="make_table",
    )(me.reshape(1), device, local, far_device, far_local)


def diagonal_kernel(parent, ranks, basis_ref, diag_ref, inverse_ref, out_ref, col_ref):
    c = pl.program_id(0)
    redundant = inverse_ref.shape[1]
    basis = basis_ref[0]
    diagonal = diag_ref[0]
    red = basis[:, :redundant]
    skel = basis[:, redundant:]
    skel_t = skel.T
    left = dot(basis.T, diagonal).astype(BF16)
    upper = dot_wide(inverse_ref[0], dot(left[:redundant], skel))
    lower = dot_wide(dot(left[redundant:], red), inverse_ref[0])
    high, low = halves(upper)
    col = (skel.astype(F32) - (dot(red, high) + dot(red, low))).astype(BF16)
    col_ref[0] = col
    high, low = halves(lower)
    row = (skel_t.astype(F32) - (dot_nt(high, red) + dot_nt(low, red))).astype(BF16)
    reduced = dot(dot(row, diagonal).astype(BF16), col)
    rank = ranks[c]
    rows_at = lax.broadcasted_iota(jnp.int32, reduced.shape, 0)
    cols_at = lax.broadcasted_iota(jnp.int32, reduced.shape, 1)
    keep = (rows_at < rank) & (cols_at < rank)
    out_ref[0] = jnp.where(keep, reduced, 0.0).astype(BF16)


def diagonal_part(bases, diag_blocks, diag_inverses, ranks, parent_group):
    local_count, block, _ = bases.shape
    redundant = diag_inverses.shape[1]
    skeleton = block - redundant

    def own(*shape):
        return pl.BlockSpec((1,) + shape, lambda c, parent, ranks: (c, 0, 0))

    return pl.pallas_call(
        diagonal_kernel,
        out_shape=(
            jax.ShapeDtypeStruct((local_count, skeleton, skeleton), BF16),
            jax.ShapeDtypeStruct((local_count, block, skeleton), BF16),
        ),
        grid_spec=pltpu.PrefetchScalarGridSpec(
            num_scalar_prefetch=2,
            grid=(local_count,),
            in_specs=[
                own(block, block),
                own(block, block),
                own(redundant, redundant),
            ],
            out_specs=[
                pl.BlockSpec(
                    (1, skeleton, skeleton), lambda c, parent, ranks: (parent[c], 0, 0)
                ),
                own(block, skeleton),
            ],
        ),
        compiler_params=pltpu.CompilerParams(vmem_limit_bytes=16 * 2**20),
        cost_estimate=pl.CostEstimate(
            flops=10**9, bytes_accessed=4 * 10**6, transcendentals=0
        ),
        name="diagonal_part",
    )(parent_group[:, 0], ranks, bases, diag_blocks, diag_inverses)


def reduce_kernel(chunk, far, *refs):
    tables_hbm = refs[:far]
    (
        me_hbm,
        ranks_hbm,
        moved_hbm,
        col,
        out_hbm,
        tables,
        me,
        ranks,
        moved,
        out,
        table_sem,
        int_sem,
        in_sem,
        out_sem,
    ) = refs[far:]
    steps = moved.shape[0] // chunk
    firsts = (
        pltpu.make_async_copy(me_hbm, me, int_sem.at[0]),
        pltpu.make_async_copy(ranks_hbm, ranks, int_sem.at[1]),
    ) + tuple(
        pltpu.make_async_copy(tables_hbm[t], tables.at[t], table_sem.at[t]) for t in range(far)
    )

    def in_copy(i):
        part = pl.ds(i * chunk, chunk)
        return pltpu.make_async_copy(moved_hbm.at[part], moved.at[part], in_sem.at[i])

    def out_copy(i):
        part = pl.ds(i * PIECE, PIECE)
        return pltpu.make_async_copy(out.at[part], out_hbm.at[part], out_sem.at[i])

    for copy in firsts:
        copy.start()
    for i in range(steps):
        in_copy(i).start()
    for copy in firsts:
        copy.wait()
    cols_at = lax.broadcasted_iota(jnp.int32, out.shape[1:], 1)
    my_z = me[0] // NEAR_LINKS

    for i in range(steps):
        in_copy(i).wait()
        for e in range(i * chunk, (i + 1) * chunk):
            source = e // CAPACITY
            apart = (source // NEAR_LINKS) ^ my_z
            column = (apart % 2) * CAPACITY + e % CAPACITY
            local = tables[apart // 2, source % NEAR_LINKS, column]
            owner = jnp.maximum(local, 0)
            rank = jnp.where(local < 0, 0, ranks[owner])
            out[e] = jnp.where(cols_at < rank, dot(moved[e], col[owner]), 0.0).astype(BF16)
            if e % PIECE == PIECE - 1:
                out_copy(e // PIECE).start()
    for i in range(moved.shape[0] // PIECE):
        out_copy(i).wait()


def reduce_blocks(moved, tables, me, col_basis, ranks):
    slots, skeleton, block = moved.shape
    far = len(tables)
    chunk = 32
    hbm = pl.BlockSpec(memory_space=pl.ANY)
    dma = pltpu.SemaphoreType.DMA
    return pl.pallas_call(
        functools.partial(reduce_kernel, chunk, far),
        out_shape=jax.ShapeDtypeStruct((slots, skeleton, skeleton), BF16),
        in_specs=[hbm] * (far + 3) + [pl.BlockSpec(memory_space=pltpu.VMEM)],
        out_specs=hbm,
        scratch_shapes=[
            pltpu.SMEM((far,) + tables[0].shape, jnp.int32),
            pltpu.SMEM((1,), jnp.int32),
            pltpu.SMEM(ranks.shape, jnp.int32),
            pltpu.VMEM(moved.shape, BF16),
            pltpu.VMEM((slots, skeleton, skeleton), BF16),
            dma((far,)),
            dma((2,)),
            dma((slots // chunk,)),
            dma((slots // PIECE,)),
        ],
        compiler_params=pltpu.CompilerParams(vmem_limit_bytes=12 * 2**20),
        cost_estimate=pl.CostEstimate(
            flops=6 * 10**8, bytes_accessed=7 * 10**6, transcendentals=0
        ),
        name="reduce_blocks",
    )(*tables, me.reshape(1), ranks, moved, col_basis)


def swap_halves(x, axis_name, size):
    whole = lax.axis_size(axis_name)
    me = lax.axis_index(axis_name)
    bit = 1
    while bit < size:
        pairs = x.reshape((size // (2 * bit), 2, bit) + x.shape[1:])
        mine = (me // bit) % 2
        kept = lax.dynamic_index_in_dim(pairs, mine, 1, keepdims=False)
        given = lax.dynamic_index_in_dim(pairs, 1 - mine, 1, keepdims=False)
        got = lax.ppermute(given, axis_name, [(i, i ^ bit) for i in range(whole)])
        low, high = jnp.stack([kept, got], 1), jnp.stack([got, kept], 1)
        x = jnp.where(mine == 0, low, high).reshape(x.shape)
        bit *= 2
    return x


def on_device(
    near_blocks, diag_blocks, bases, diag_inverses, col_device, col_local, ranks, parent_group
):
    buckets = lax.axis_size("clu")
    local_count = ranks.shape[0]
    me = lax.axis_index("clu")
    across = [(i, i ^ NEAR_LINKS) for i in range(buckets)]
    far_device = lax.ppermute(col_device, "clu", across)
    far_local = lax.ppermute(col_local, "clu", across)
    send = move_blocks(
        near_blocks, diag_blocks, bases, diag_inverses, col_device, ranks, buckets
    )
    send, far_device, far_local = lax.optimization_barrier((send, far_device, far_local))
    skeleton, block = send.shape[1:]
    received = lax.all_to_all(
        send.reshape(buckets, CAPACITY, skeleton, block), "clu", 0, 0, tiled=True
    )
    outgoing, col_basis = diagonal_part(
        bases, diag_blocks, diag_inverses, ranks, parent_group
    )
    arrived = swap_halves(outgoing, "grp", lax.axis_size("grp"))
    merged = arrived.reshape(local_count // 2, 2, skeleton, skeleton)

    table = make_table(me, col_device, col_local, far_device, far_local, buckets)
    table = swap_halves(table, "clu", NEAR_LINKS)
    table, merged = lax.optimization_barrier((table, merged))
    table = table[:, : 2 * HALF_Z * CAPACITY].reshape(NEAR_LINKS, 2, HALF_Z, CAPACITY)
    my_place = me // (2 * NEAR_LINKS)
    tables = []
    for apart in range(HALF_Z):
        given = lax.dynamic_index_in_dim(table, my_place ^ apart, 2, keepdims=False)
        given = given.reshape(NEAR_LINKS, 2 * CAPACITY)
        if apart:
            pairs = [(i, i ^ (2 * apart * NEAR_LINKS)) for i in range(buckets)]
            given = lax.ppermute(given, "clu", pairs)
        tables.append(given)
    reduced = reduce_blocks(
        received.reshape(buckets * CAPACITY, skeleton, block), tables, me, col_basis, ranks
    )
    return reduced.reshape(1, buckets, CAPACITY, skeleton, skeleton), merged


def solution(mesh):
    in_specs = (
        P(("grp", "clu"), None, None, None),
        P(("grp", "clu"), None, None),
        P(("grp", "clu"), None, None),
        P(("grp", "clu"), None, None),
        P(("grp", "clu"), None),
        P(("grp", "clu"), None),
        P(("grp", "clu")),
        P(("grp", "clu"), None),
    )
    out_specs = (P(("grp", "clu"), None, None, None, None), P(("grp", "clu"), None, None, None))
    return jax.shard_map(
        on_device, mesh=mesh, in_specs=in_specs, out_specs=out_specs, check_vma=False
    )
```

```python
import functools

import jax
import jax.numpy as jnp
from jax import lax
from jax.experimental import pallas as pl
from jax.experimental.pallas import tpu as pltpu
from jax.sharding import PartitionSpec as P

BF16 = jnp.bfloat16
F32 = jnp.float32
CAPACITY = 2
PIECE = 8
NEAR_LINKS = 4
HALF_Z = 4


def dot(a, b):
    return jnp.dot(a, b, preferred_element_type=F32)


def dot_nt(a, b):
    return lax.dot_general(a, b, (((1,), (1,)), ((), ())), preferred_element_type=F32)


def halves(x):
    high = x.astype(BF16)
    return high, (x - high.astype(F32)).astype(BF16)


def dot_wide(a, b):
    a_high, a_low = halves(a)
    b_high, b_low = halves(b)
    upper = jnp.concatenate([b_high, b_low], 1)
    lower = jnp.concatenate([b_high, jnp.zeros_like(b_low)], 1)
    both = dot(jnp.concatenate([a_high, a_low], 1), jnp.concatenate([upper, lower], 0))
    return both[:, : b.shape[1]] + both[:, b.shape[1] :]


def move_kernel(
    near_count,
    groups,
    targets_hbm,
    ranks_hbm,
    bases_hbm,
    diag_hbm,
    inverse_hbm,
    near_hbm,
    send_hbm,
    targets,
    ranks,
    bases,
    diag,
    inverse,
    near,
    rows,
    moved,
    count,
    place,
    int_sem,
    in_sem,
    near_sem,
    out_sem,
):
    local_count, block, _ = bases.shape
    redundant = inverse.shape[1]
    skeleton = block - redundant
    members = []
    for size in groups:
        first = members[-1][-1] + 1 if members else 0
        members.append(range(first, first + size))
    ints = (
        pltpu.make_async_copy(targets_hbm, targets, int_sem.at[0]),
        pltpu.make_async_copy(ranks_hbm, ranks, int_sem.at[1]),
    )

    def part(g):
        return pl.ds(members[g][0], len(members[g]))

    def inputs(g):
        return (
            pltpu.make_async_copy(bases_hbm.at[part(g)], bases.at[part(g)], in_sem.at[g, 0]),
            pltpu.make_async_copy(diag_hbm.at[part(g)], diag.at[part(g)], in_sem.at[g, 1]),
            pltpu.make_async_copy(inverse_hbm.at[part(g)], inverse.at[part(g)], in_sem.at[g, 2]),
        )

    def near_copy(g):
        return pltpu.make_async_copy(near_hbm.at[part(g)], near.at[part(g)], near_sem.at[g])

    def out_copy(c, k):
        return pltpu.make_async_copy(moved.at[c, k], send_hbm.at[place[c, k]], out_sem.at[c, k])

    for g in range(len(groups)):
        for copy in inputs(g):
            copy.start()
        if g == 0:
            for copy in ints:
                copy.start()
        near_copy(g).start()

    def clear(d, carry):
        count[d] = 0
        return carry

    lax.fori_loop(0, count.shape[0], clear, 0)
    for copy in ints:
        copy.wait()

    def assign(l, carry):
        for k in range(near_count):
            d = targets[l, k]
            place[l, k] = d * CAPACITY + count[d]
            count[d] = count[d] + 1
        return carry

    lax.fori_loop(0, local_count, assign, 0)

    def prepare(g):
        red = [bases[c][:, :redundant] for c in members[g]]
        skel_t = [bases[c][:, redundant:].T for c in members[g]]
        left = [dot(s, diag[c]).astype(BF16) for s, c in zip(skel_t, members[g])]
        factor = [dot(l, r) for l, r in zip(left, red)]
        lower = [halves(dot_wide(f, inverse[c])) for f, c in zip(factor, members[g])]
        taken = [
            dot_nt(jnp.concatenate(pair, 1), jnp.concatenate([r, r], 1))
            for pair, r in zip(lower, red)
        ]
        for c, s, t in zip(members[g], skel_t, taken):
            rows[c] = (s.astype(F32) - t).astype(BF16)

    rows_at = lax.broadcasted_iota(jnp.int32, (skeleton, block), 0)

    def move(g):
        for c in members[g]:
            keep = rows_at < ranks[c]
            row = rows[c]
            for k in range(near_count):
                moved[c, k] = jnp.where(keep, dot(row, near[c, k]), 0.0).astype(BF16)
            for k in range(near_count):
                out_copy(c, k).start()

    def finish_one(c, carry):
        for k in range(near_count):
            out_copy(c, k).wait()
        return carry

    for copy in inputs(0):
        copy.wait()
    prepare(0)
    for g in range(len(groups)):
        near_copy(g).wait()
        if g + 1 < len(groups):
            for copy in inputs(g + 1):
                copy.wait()
        move(g)
        if g + 1 < len(groups):
            prepare(g + 1)
    lax.fori_loop(0, local_count, finish_one, 0)


def move_blocks(near_blocks, diag_blocks, bases, diag_inverses, col_device, ranks, buckets):
    local_count, near_count, block, _ = near_blocks.shape
    redundant = diag_inverses.shape[1]
    skeleton = block - redundant
    groups = (4, 4)
    hbm = pl.BlockSpec(memory_space=pl.ANY)
    dma = pltpu.SemaphoreType.DMA
    return pl.pallas_call(
        functools.partial(move_kernel, near_count, groups),
        out_shape=jax.ShapeDtypeStruct((buckets * CAPACITY, skeleton, block), BF16),
        in_specs=[hbm] * 6,
        out_specs=hbm,
        scratch_shapes=[
            pltpu.SMEM((local_count, near_count), jnp.int32),
            pltpu.SMEM((local_count,), jnp.int32),
            pltpu.VMEM((local_count, block, block), BF16),
            pltpu.VMEM((local_count, block, block), BF16),
            pltpu.VMEM((local_count, redundant, redundant), F32),
            pltpu.VMEM((local_count, near_count, block, block), BF16),
            pltpu.VMEM((local_count, skeleton, block), BF16),
            pltpu.VMEM((local_count, near_count, skeleton, block), BF16),
            pltpu.SMEM((buckets,), jnp.int32),
            pltpu.SMEM((local_count, near_count), jnp.int32),
            dma((2,)),
            dma((len(groups), 3)),
            dma((len(groups),)),
            dma((local_count, near_count)),
        ],
        compiler_params=pltpu.CompilerParams(vmem_limit_bytes=56 * 2**20),
        cost_estimate=pl.CostEstimate(
            flops=2 * 10**9, bytes_accessed=13 * 10**6, transcendentals=0
        ),
        name="move_blocks",
    )(col_device, ranks, bases, diag_blocks, diag_inverses, near_blocks)


def table_kernel(me, *refs):
    inputs, table, held, count, sem = refs[:4], refs[4], refs[5:9], refs[9], refs[10]
    copies = [
        pltpu.make_async_copy(ref, place, sem.at[i])
        for i, (ref, place) in enumerate(zip(inputs, held))
    ]
    for copy in copies:
        copy.start()
    device, local, far_device, far_local = held
    local_count, near_count = device.shape
    half = HALF_Z * CAPACITY * 2
    my_side = (me[0] // NEAR_LINKS) % 2

    def blank(x, carry):
        for j in range(2 * half):
            table[x, j] = -1
        return carry

    lax.fori_loop(0, NEAR_LINKS, blank, 0)
    for copy in copies:
        copy.wait()
    for whose, (devices, locals_) in enumerate(((device, local), (far_device, far_local))):

        def clear(d, carry):
            count[d] = 0
            return carry

        def assign(l, carry):
            for k in range(near_count):
                d = devices[l, k]
                z = d // NEAR_LINKS
                away = jnp.where(z % 2 == my_side, 0, half)
                slot = count[d]
                count[d] = slot + 1
                column = (whose * HALF_Z + z // 2) * CAPACITY + slot + away
                table[d % NEAR_LINKS, column] = locals_[l, k]
            return carry

        lax.fori_loop(0, count.shape[0], clear, 0)
        lax.fori_loop(0, local_count, assign, 0)


def make_table(me, device, local, far_device, far_local, buckets):
    smem = pl.BlockSpec(memory_space=pltpu.SMEM)
    hbm = pl.BlockSpec(memory_space=pl.ANY)
    return pl.pallas_call(
        table_kernel,
        out_shape=jax.ShapeDtypeStruct((NEAR_LINKS, HALF_Z * CAPACITY * 4), jnp.int32),
        in_specs=[smem] + [hbm] * 4,
        out_specs=smem,
        scratch_shapes=[pltpu.SMEM(device.shape, jnp.int32)] * 4
        + [pltpu.SMEM((buckets,), jnp.int32), pltpu.SemaphoreType.DMA((4,))],
        compiler_params=pltpu.CompilerParams(vmem_limit_bytes=16 * 2**20),
        name="make_table",
    )(me.reshape(1), device, local, far_device, far_local)


def diagonal_kernel(parent, ranks, basis_ref, diag_ref, inverse_ref, out_ref, col_ref):
    c = pl.program_id(0)
    redundant = inverse_ref.shape[1]
    basis = basis_ref[0]
    diagonal = diag_ref[0]
    red = basis[:, :redundant]
    skel = basis[:, redundant:]
    skel_t = skel.T
    left = dot(basis.T, diagonal).astype(BF16)
    upper = dot_wide(inverse_ref[0], dot(left[:redundant], skel))
    lower = dot_wide(dot(left[redundant:], red), inverse_ref[0])
    high, low = halves(upper)
    col = (skel.astype(F32) - (dot(red, high) + dot(red, low))).astype(BF16)
    col_ref[0] = col
    high, low = halves(lower)
    row = (skel_t.astype(F32) - (dot_nt(high, red) + dot_nt(low, red))).astype(BF16)
    reduced = dot(dot(row, diagonal).astype(BF16), col)
    rank = ranks[c]
    rows_at = lax.broadcasted_iota(jnp.int32, reduced.shape, 0)
    cols_at = lax.broadcasted_iota(jnp.int32, reduced.shape, 1)
    keep = (rows_at < rank) & (cols_at < rank)
    out_ref[0] = jnp.where(keep, reduced, 0.0).astype(BF16)


def diagonal_part(bases, diag_blocks, diag_inverses, ranks, parent_group):
    local_count, block, _ = bases.shape
    redundant = diag_inverses.shape[1]
    skeleton = block - redundant

    def own(*shape):
        return pl.BlockSpec((1,) + shape, lambda c, parent, ranks: (c, 0, 0))

    return pl.pallas_call(
        diagonal_kernel,
        out_shape=(
            jax.ShapeDtypeStruct((local_count, skeleton, skeleton), BF16),
            jax.ShapeDtypeStruct((local_count, block, skeleton), BF16),
        ),
        grid_spec=pltpu.PrefetchScalarGridSpec(
            num_scalar_prefetch=2,
            grid=(local_count,),
            in_specs=[
                own(block, block),
                own(block, block),
                own(redundant, redundant),
            ],
            out_specs=[
                pl.BlockSpec(
                    (1, skeleton, skeleton), lambda c, parent, ranks: (parent[c], 0, 0)
                ),
                own(block, skeleton),
            ],
        ),
        compiler_params=pltpu.CompilerParams(vmem_limit_bytes=16 * 2**20),
        cost_estimate=pl.CostEstimate(
            flops=10**9, bytes_accessed=4 * 10**6, transcendentals=0
        ),
        name="diagonal_part",
    )(parent_group[:, 0], ranks, bases, diag_blocks, diag_inverses)


def reduce_kernel(chunk, far, *refs):
    tables_hbm = refs[:far]
    (
        me_hbm,
        ranks_hbm,
        moved_hbm,
        col_hbm,
        out_hbm,
        tables,
        me,
        ranks,
        moved,
        col,
        out,
        table_sem,
        int_sem,
        in_sem,
        out_sem,
    ) = refs[far:]
    steps = moved.shape[0] // chunk
    firsts = (
        pltpu.make_async_copy(me_hbm, me, int_sem.at[0]),
        pltpu.make_async_copy(ranks_hbm, ranks, int_sem.at[1]),
        pltpu.make_async_copy(col_hbm, col, int_sem.at[2]),
    ) + tuple(
        pltpu.make_async_copy(tables_hbm[t], tables.at[t], table_sem.at[t]) for t in range(far)
    )

    def in_copy(i):
        part = pl.ds(i * chunk, chunk)
        return pltpu.make_async_copy(moved_hbm.at[part], moved.at[part], in_sem.at[i])

    def out_copy(i):
        part = pl.ds(i * PIECE, PIECE)
        return pltpu.make_async_copy(out.at[part], out_hbm.at[part], out_sem.at[i])

    for copy in firsts:
        copy.start()
    for i in range(steps):
        in_copy(i).start()
    for copy in firsts:
        copy.wait()
    cols_at = lax.broadcasted_iota(jnp.int32, out.shape[1:], 1)
    my_z = me[0] // NEAR_LINKS

    for i in range(steps):
        in_copy(i).wait()
        for e in range(i * chunk, (i + 1) * chunk):
            source = e // CAPACITY
            apart = (source // NEAR_LINKS) ^ my_z
            column = (apart % 2) * CAPACITY + e % CAPACITY
            local = tables[apart // 2, source % NEAR_LINKS, column]
            owner = jnp.maximum(local, 0)
            rank = jnp.where(local < 0, 0, ranks[owner])
            out[e] = jnp.where(cols_at < rank, dot(moved[e], col[owner]), 0.0).astype(BF16)
            if e % PIECE == PIECE - 1:
                out_copy(e // PIECE).start()
    for i in range(moved.shape[0] // PIECE):
        out_copy(i).wait()


def reduce_blocks(moved, tables, me, col_basis, ranks):
    slots, skeleton, block = moved.shape
    far = len(tables)
    chunk = 32
    hbm = pl.BlockSpec(memory_space=pl.ANY)
    dma = pltpu.SemaphoreType.DMA
    return pl.pallas_call(
        functools.partial(reduce_kernel, chunk, far),
        out_shape=jax.ShapeDtypeStruct((slots, skeleton, skeleton), BF16),
        in_specs=[hbm] * (far + 4),
        out_specs=hbm,
        scratch_shapes=[
            pltpu.SMEM((far,) + tables[0].shape, jnp.int32),
            pltpu.SMEM((1,), jnp.int32),
            pltpu.SMEM(ranks.shape, jnp.int32),
            pltpu.VMEM(moved.shape, BF16),
            pltpu.VMEM(col_basis.shape, BF16),
            pltpu.VMEM((slots, skeleton, skeleton), BF16),
            dma((far,)),
            dma((3,)),
            dma((slots // chunk,)),
            dma((slots // PIECE,)),
        ],
        compiler_params=pltpu.CompilerParams(vmem_limit_bytes=12 * 2**20),
        cost_estimate=pl.CostEstimate(
            flops=6 * 10**8, bytes_accessed=7 * 10**6, transcendentals=0
        ),
        name="reduce_blocks",
    )(*tables, me.reshape(1), ranks, moved, col_basis)


def swap_halves(x, axis_name, size):
    whole = lax.axis_size(axis_name)
    me = lax.axis_index(axis_name)
    bit = 1
    while bit < size:
        pairs = x.reshape((size // (2 * bit), 2, bit) + x.shape[1:])
        mine = (me // bit) % 2
        kept = lax.dynamic_index_in_dim(pairs, mine, 1, keepdims=False)
        given = lax.dynamic_index_in_dim(pairs, 1 - mine, 1, keepdims=False)
        got = lax.ppermute(given, axis_name, [(i, i ^ bit) for i in range(whole)])
        low, high = jnp.stack([kept, got], 1), jnp.stack([got, kept], 1)
        x = jnp.where(mine == 0, low, high).reshape(x.shape)
        bit *= 2
    return x


def on_device(
    near_blocks, diag_blocks, bases, diag_inverses, col_device, col_local, ranks, parent_group
):
    buckets = lax.axis_size("clu")
    local_count = ranks.shape[0]
    me = lax.axis_index("clu")
    across = [(i, i ^ NEAR_LINKS) for i in range(buckets)]
    far_device = lax.ppermute(col_device, "clu", across)
    far_local = lax.ppermute(col_local, "clu", across)
    send = move_blocks(
        near_blocks, diag_blocks, bases, diag_inverses, col_device, ranks, buckets
    )
    send, far_device, far_local = lax.optimization_barrier((send, far_device, far_local))
    skeleton, block = send.shape[1:]
    received = lax.all_to_all(
        send.reshape(buckets, CAPACITY, skeleton, block), "clu", 0, 0, tiled=True
    )
    outgoing, col_basis = diagonal_part(
        bases, diag_blocks, diag_inverses, ranks, parent_group
    )
    arrived = swap_halves(outgoing, "grp", lax.axis_size("grp"))
    merged = arrived.reshape(local_count // 2, 2, skeleton, skeleton)

    table = make_table(me, col_device, col_local, far_device, far_local, buckets)
    table = swap_halves(table, "clu", NEAR_LINKS)
    table, merged = lax.optimization_barrier((table, merged))
    table = table[:, : 2 * HALF_Z * CAPACITY].reshape(NEAR_LINKS, 2, HALF_Z, CAPACITY)
    my_place = me // (2 * NEAR_LINKS)
    tables = [None] * HALF_Z
    for apart in (2, 3, 1, 0):
        given = lax.dynamic_index_in_dim(table, my_place ^ apart, 2, keepdims=False)
        given = given.reshape(NEAR_LINKS, 2 * CAPACITY)
        if apart:
            pairs = [(i, i ^ (2 * apart * NEAR_LINKS)) for i in range(buckets)]
            given = lax.ppermute(given, "clu", pairs)
        tables[apart] = given
    reduced = reduce_blocks(
        received.reshape(buckets * CAPACITY, skeleton, block), tables, me, col_basis, ranks
    )
    return reduced.reshape(1, buckets, CAPACITY, skeleton, skeleton), merged


def solution(mesh):
    in_specs = (
        P(("grp", "clu"), None, None, None),
        P(("grp", "clu"), None, None),
        P(("grp", "clu"), None, None),
        P(("grp", "clu"), None, None),
        P(("grp", "clu"), None),
        P(("grp", "clu"), None),
        P(("grp", "clu")),
        P(("grp", "clu"), None),
    )
    out_specs = (P(("grp", "clu"), None, None, None, None), P(("grp", "clu"), None, None, None))
    return jax.shard_map(
        on_device, mesh=mesh, in_specs=in_specs, out_specs=out_specs, check_vma=False
    )
```
